32 devices in a mesh: dp: 8 (over z, x), fsdp: 4 (over y, core).
Axes of the slice: x: 2, y: 2, z: 4, core: 2. Of those that a mesh axis runs over, the one named last changes fastest.
Arguments:
- hidden_in: bfloat16 [2, 8, 256, 2048], P(None, 'dp', 'fsdp'), may hold values from -6 to 6
- seq_lengths: int32 [2, 8], P(None, 'dp'), may hold values from 64 to 256, as said below
- out_grad: bfloat16 [2, 8, 256, 2048], P(None, 'dp', 'fsdp'), may hold values from -6 to 6
- attn_gain: bfloat16 [2048], P(('dp', 'fsdp')), may hold values from 0.5 to 1.5
- w_query: bfloat16 [2048, 2048], P(('dp', 'fsdp')), may hold values from -0.125 to 0.125
- key_matrix: bfloat16 [2048, 1024], P(('dp', 'fsdp')), may hold values from -0.125 to 0.125
- value_matrix: bfloat16 [2048, 1024], P(('dp', 'fsdp')), may hold values from -0.125 to 0.125
- w_out: bfloat16 [2048, 2048], P(('dp', 'fsdp')), may hold values from -0.5 to 0.5
- mlp_gain: bfloat16 [2048], P(('dp', 'fsdp')), may hold values from 0.5 to 1.5
- w_gate: bfloat16 [2048, 8192], P(('dp', 'fsdp')), may hold values from -0.125 to 0.125
- w_up: bfloat16 [2048, 8192], P(('dp', 'fsdp')), may hold values from -0.125 to 0.125
- w_down: bfloat16 [2048, 8192], P(('dp', 'fsdp')), may hold values from -0.09375 to 0.09375
Outputs:
- hidden_out: bfloat16 [2, 8, 256, 2048], P(None, 'dp', 'fsdp')
- in_grad: bfloat16 [2, 8, 256, 2048], P(None, 'dp', 'fsdp')
- grad_attn_gain: float32 [2048], P(('dp', 'fsdp'))
- grad_query: float32 [2048, 2048], P(('dp', 'fsdp'))
- grad_key: float32 [2048, 1024], P(('dp', 'fsdp'))
- grad_value: float32 [2048, 1024], P(('dp', 'fsdp'))
- grad_out: float32 [2048, 2048], P(('dp', 'fsdp'))
- grad_mlp_gain: float32 [2048], P(('dp', 'fsdp'))
- grad_gate: float32 [2048, 8192], P(('dp', 'fsdp'))
- grad_up: float32 [2048, 8192], P(('dp', 'fsdp'))
- grad_down: float32 [2048, 8192], P(('dp', 'fsdp'))
The draws below stay inside these ranges and needn't reach their ends.
Inputs may be any that keep to these rules, and one draw needn't show every extreme that they name: Slots at or past seq_lengths are padding; in every draw some sequence has all 256 slots live and some has 64.
All inputs are finite; a program needn't handle non-finite values.
Results may differ from the reference program's by a relative error of at most 0.015.
Values may be sent and summed in bfloat16 or wider, within the bound.
No kernel may reach another device: no remote copies, remote signals or barrier semaphores. Data moves between devices by JAX's collectives and lax.ppermute only.
A program may use at most 896 MiB of HBM per device.

```python
import math
import jax
import jax.numpy as jnp
from jax import lax

MODEL_WIDTH = 2048
QUERY_HEADS = 8
KEY_VALUE_HEADS = 4
HEAD_DIMENSION = 256
FF = 8192
MICRO = 2
BATCH = 8
SEQ = 256


def draw_seq_lengths(key, part):
    first_key, pick_key, other_key = jax.random.split(key, 3)
    count_all = MICRO * BATCH
    draw_lengths = jax.random.randint(first_key, (MICRO, BATCH), SEQ // 4, SEQ + 1, dtype=jnp.int32)
    slot_index = jnp.arange(count_all, dtype=jnp.int32).reshape(MICRO, BATCH)
    longest = jax.random.randint(pick_key, (), 0, count_all, dtype=jnp.int32)
    shortest = (longest + 1 + jax.random.randint(other_key, (), 0, count_all - 1, dtype=jnp.int32)) % count_all
    draw_lengths = jnp.where(slot_index == longest, SEQ, jnp.where(slot_index == shortest, SEQ // 4, draw_lengths))
    return draw_lengths.astype(jnp.int32)


def shard_levels(own_key, shape, shards, least, largest):
    def one(dim, parts):
        draws = jax.random.uniform(jax.random.fold_in(jax.random.fold_in(own_key, 6), dim), (parts,), jnp.float32, least / len(shards), largest / len(shards))
        return jnp.repeat(jnp.exp(draws), shape[dim] // parts).reshape((-1,) + (1,) * (len(shape) - dim - 1))

    factor_of = one(*shards[0])
    for cut in shards[1:]:
        factor_of = factor_of * one(*cut)
    return factor_of


def gaussian(rng, extent, deviation, limit, shards=(), held_as=jnp.bfloat16):
    level = shard_levels(rng, extent, shards, -0.22, 0.18) if shards else 1.0
    entries = jax.random.normal(rng, extent, jnp.float32) * deviation * level
    return jnp.minimum(jnp.maximum(entries, -limit), limit).astype(held_as)


def setup_inputs(seed: int = 0) -> dict:
    arg_keys = jax.random.split(jax.random.key(seed), 13)
    hidden_in = gaussian(arg_keys[0], (MICRO, BATCH, SEQ, MODEL_WIDTH), 1.0, 6.0, ((1, 8), (2, 4)))
    seq_lengths = draw_seq_lengths(jax.random.fold_in(arg_keys[12], 71), 0)
    out_grad = gaussian(arg_keys[2], (MICRO, BATCH, SEQ, MODEL_WIDTH), 1.0, 6.0, ((1, 8), (2, 4)))
    attn_gain = jnp.clip(1.0 + 0.1 * jax.random.normal(arg_keys[3], (MODEL_WIDTH,), jnp.float32), 0.5, 1.5).astype(jnp.bfloat16)
    w_query = gaussian(arg_keys[4], (MODEL_WIDTH, QUERY_HEADS * HEAD_DIMENSION), MODEL_WIDTH ** -0.5, 0.125, ((0, 32),))
    key_matrix = gaussian(arg_keys[5], (MODEL_WIDTH, KEY_VALUE_HEADS * HEAD_DIMENSION), MODEL_WIDTH ** -0.5, 0.125, ((0, 32),))
    value_matrix = gaussian(arg_keys[6], (MODEL_WIDTH, KEY_VALUE_HEADS * HEAD_DIMENSION), MODEL_WIDTH ** -0.5, 0.125, ((0, 32),))
    w_out = gaussian(arg_keys[7], (MODEL_WIDTH, QUERY_HEADS * HEAD_DIMENSION), (QUERY_HEADS * HEAD_DIMENSION // 16) ** -0.5, 0.5, ((0, 32),))
    mlp_gain = jnp.clip(1.0 + 0.1 * jax.random.normal(arg_keys[8], (MODEL_WIDTH,), jnp.float32), 0.5, 1.5).astype(jnp.bfloat16)
    w_gate = gaussian(arg_keys[9], (MODEL_WIDTH, FF), MODEL_WIDTH ** -0.5, 0.125, ((0, 32),))
    w_up = gaussian(arg_keys[10], (MODEL_WIDTH, FF), MODEL_WIDTH ** -0.5, 0.125, ((0, 32),))
    w_down = gaussian(arg_keys[11], (MODEL_WIDTH, FF), (FF // 2) ** -0.5, 0.09375, ((0, 32),))
    return {"hidden_in": hidden_in, "seq_lengths": seq_lengths, "out_grad": out_grad, "attn_gain": attn_gain, "w_query": w_query, "key_matrix": key_matrix, "value_matrix": value_matrix, "w_out": w_out, "mlp_gain": mlp_gain, "w_gate": w_gate, "w_up": w_up, "w_down": w_down}


EPS_NORM = 1e-06
ROPE_BASE = 1000042.0
NEG_FILL = -1e+30
HIGHEST = lax.Precision.HIGHEST

@jax.custom_vjp
def begin_offset(v):
    return lax.optimization_barrier(v.astype(jnp.bfloat16)).astype(jnp.float32)

@jax.custom_vjp
def low_back(v):
    return v

def low_keep(v):
    return (begin_offset(v), None)

def low_pass(kept, grad):
    return (grad,)

def back_keep(v):
    return (v, None)

def back_low(kept, grad):
    return (begin_offset(grad),)
begin_offset.defvjp(low_keep, low_pass)
low_back.defvjp(back_keep, back_low)

def rope_tables(positions, head_size):
    half_size = head_size // 2
    inverse = ROPE_BASE ** (-(jnp.arange(half_size, dtype=jnp.float32) * 2.0 / head_size))
    angles = positions.astype(jnp.float32)[:, None] * inverse[None, :]
    angles = jnp.concatenate([angles, angles], axis=-1)
    return (jnp.cos(angles), jnp.sin(angles))

def rotate_half(value_rows):
    half_size = value_rows.shape[-1] // 2
    return jnp.concatenate([-value_rows[..., half_size:], value_rows[..., :half_size]], axis=-1)

def rotary_embed(value_rows, cosine_table, sine_table):
    return value_rows * cosine_table + rotate_half(value_rows) * sine_table

def rms_normed(value_rows):
    return value_rows * lax.rsqrt(lax.optimization_barrier(jnp.mean(value_rows * value_rows, axis=-1, keepdims=True)) + EPS_NORM)

def layer_forward(params, inputs, lengths):
    attn_gain, w_query, key_matrix, value_matrix, w_out, mlp_gain, w_gate, w_up, w_down = params
    current_group = inputs.shape[0]
    sequence_length = inputs.shape[1]
    positions = jnp.arange(sequence_length, dtype=jnp.int32)
    cosine_table, sine_table = rope_tables(positions, HEAD_DIMENSION)
    cosine_table = cosine_table[:, None, :]
    sine_table = sine_table[:, None, :]
    valid = positions[None, :] < lengths[:, None]
    mask_rows = valid.astype(jnp.float32)[:, :, None]
    first_normalized = begin_offset(rms_normed(inputs) * attn_gain)
    query_rows = low_back(jnp.einsum('gtd,de->gte', first_normalized, w_query, precision=HIGHEST))
    query_rows = begin_offset(rotary_embed(query_rows.reshape(current_group, sequence_length, QUERY_HEADS, HEAD_DIMENSION), cosine_table, sine_table))
    query_rows = query_rows.reshape(current_group, sequence_length, KEY_VALUE_HEADS, QUERY_HEADS // KEY_VALUE_HEADS, HEAD_DIMENSION)
    key_rows = low_back(jnp.einsum('gtd,de->gte', first_normalized, key_matrix, precision=HIGHEST))
    key_rows = begin_offset(rotary_embed(key_rows.reshape(current_group, sequence_length, KEY_VALUE_HEADS, HEAD_DIMENSION), cosine_table, sine_table))
    value_rows = begin_offset(low_back(jnp.einsum('gtd,de->gte', first_normalized, value_matrix, precision=HIGHEST)))
    value_rows = value_rows.reshape(current_group, sequence_length, KEY_VALUE_HEADS, HEAD_DIMENSION)
    scale = HEAD_DIMENSION ** (-0.5)
    scores = low_back(jnp.einsum('gqkjd,gskd->gkjqs', query_rows, key_rows, precision=HIGHEST) * scale)
    allowed = (positions[None, :] <= positions[:, None])[None, :, :] & valid[:, None, :]
    allowed = allowed[:, None, None, :, :]
    scores = jnp.where(allowed, scores, NEG_FILL)
    top_score = lax.optimization_barrier(jnp.max(scores, axis=-1, keepdims=True))
    log_total = top_score + jnp.log(lax.optimization_barrier(jnp.sum(jnp.exp(scores - top_score), axis=-1, keepdims=True)))
    weights = jnp.where(allowed, jnp.exp(scores - log_total), 0.0)
    mixed = jnp.einsum('gkjqs,gskd->gqkjd', begin_offset(weights), value_rows, precision=HIGHEST)
    mixed = begin_offset(low_back(mixed)).reshape(current_group, sequence_length, QUERY_HEADS * HEAD_DIMENSION)
    branch = low_back(jnp.einsum('gte,de->gtd', mixed, w_out, precision=HIGHEST))
    residual_middle = inputs + branch
    second_normalized = begin_offset(rms_normed(residual_middle) * mlp_gain)
    gate = low_back(jnp.einsum('gtd,df->gtf', second_normalized, w_gate, precision=HIGHEST))
    up_proj = low_back(jnp.einsum('gtd,df->gtf', second_normalized, w_up, precision=HIGHEST))
    hidden = begin_offset(jax.nn.silu(gate) * up_proj)
    feed = low_back(jnp.einsum('gtf,df->gtd', hidden, w_down, precision=HIGHEST))
    return mask_rows * (residual_middle + feed)

def reference(hidden_in, seq_lengths, out_grad, attn_gain, w_query, key_matrix, value_matrix, w_out, mlp_gain, w_gate, w_up, w_down):
    params = tuple((weight_arg.astype(jnp.float32) for weight_arg in (attn_gain, w_query, key_matrix, value_matrix, w_out, mlp_gain, w_gate, w_up, w_down)))
    total_seqs = MICRO * BATCH
    group_size = math.gcd(total_seqs, max(1, 4096 // SEQ))
    step_count = total_seqs // group_size
    inputs = hidden_in.astype(jnp.float32).reshape(step_count, group_size, SEQ, MODEL_WIDTH)
    cotangents = out_grad.astype(jnp.float32).reshape(step_count, group_size, SEQ, MODEL_WIDTH)
    lengths = seq_lengths.astype(jnp.int32).reshape(step_count, group_size)

    def one_group(grad_sums, entry):
        group_in, group_cot, group_len = entry

        def local_layer(weights, value_rows):
            return layer_forward(weights, value_rows, group_len)
        result, pullback = jax.vjp(local_layer, params, group_in)
        weight_grads, input_grad = pullback(group_cot)
        grad_sums = jax.tree.map(lambda a, b: a + b, grad_sums, weight_grads)
        return (grad_sums, (result.astype(jnp.bfloat16), input_grad.astype(jnp.bfloat16)))
    zero_sums = tuple((jnp.zeros_like(weight_arg) for weight_arg in params))
    grad_sums, produced = lax.scan(one_group, zero_sums, (inputs, cotangents, lengths))
    outputs = produced[0].reshape(MICRO, BATCH, SEQ, MODEL_WIDTH)
    input_grads = produced[1].reshape(MICRO, BATCH, SEQ, MODEL_WIDTH)
    return (outputs, input_grads, grad_sums[0], grad_sums[1], grad_sums[2], grad_sums[3], grad_sums[4], grad_sums[5], grad_sums[6], grad_sums[7], grad_sums[8])
```

```python
import jax
import jax.numpy as jnp
from jax import lax
from jax.sharding import Mesh, PartitionSpec as P

QUERY_HEADS = 8
KEY_VALUE_HEADS = 4
HEAD_DIMENSION = 256

EPS_NORM = 1e-06
ROPE_BASE = 1000042.0
NEG_FILL = -1e30

BF = jnp.bfloat16
F32 = jnp.float32


def rope_tables(positions, head_size):
    half_size = head_size // 2
    inverse = ROPE_BASE ** (-(jnp.arange(half_size, dtype=F32) * 2.0 / head_size))
    angles = positions.astype(F32)[:, None] * inverse[None, :]
    return jnp.cos(angles), jnp.sin(angles)


def rotary_embed(rows, cosine, sine):
    half = rows.shape[-1] // 2
    first, second = rows[..., :half], rows[..., half:]
    return jnp.concatenate(
        [first * cosine - second * sine, second * cosine + first * sine], axis=-1
    )


def rotary_backward(grads, cosine, sine):
    half = grads.shape[-1] // 2
    first, second = grads[..., :half], grads[..., half:]
    return jnp.concatenate(
        [first * cosine + second * sine, second * cosine - first * sine], axis=-1
    )


def norm_backward(normalized, reciprocal, gradient):
    return reciprocal * (
        gradient - normalized * jnp.mean(gradient * normalized, axis=-1, keepdims=True)
    )


def dot(left, right):
    return jnp.dot(left, right, preferred_element_type=F32)


def dot_right(left, right):
    return lax.dot_general(left, right, (((1,), (1,)), ((), ())), preferred_element_type=F32)


def dot_rows(left, right):
    return lax.dot_general(left, right, (((0,), (0,)), ((), ())), preferred_element_type=F32)


def swap(value, axis):
    return lax.ppermute(value, axis, [(0, 1), (1, 0)])


def ring(value, size):
    return lax.ppermute(value, "z", [(i, (i + 1) % size) for i in range(size)])


def pick(value, index, axis=0):
    return lax.dynamic_index_in_dim(value, index, axis, keepdims=False)


def put(buffer, piece, *index):
    piece = piece.reshape((1,) * len(index) + piece.shape)
    starts = tuple(index) + (0,) * (buffer.ndim - len(index))
    return lax.dynamic_update_slice(buffer, piece, starts)


def gather_yc(block):
    across = swap(block, "y")
    return [block, swap(block, "c"), across, swap(across, "c")]


def scatter_yc(parts):
    near = [parts[0].astype(F32) + swap(parts[1], "c"), parts[2].astype(F32) + swap(parts[3], "c")]
    return near[0] + swap(near[1].astype(BF), "y")


def gather_z(block, size):
    blocks = [block]
    for _ in range(size - 1):
        blocks.append(ring(blocks[-1], size))
    return blocks


def gather_zy(block, size):
    return [[b, swap(b, "y")] for b in gather_z(block, size)]


def scatter_z(parts, partners, axis, size):
    dtype = partners[0].dtype
    total = None
    for step in range(size):
        s = (step + 1) % size
        own = parts[s].astype(F32) + swap(partners[s], axis)
        total = own if total is None else own + ring(total.astype(dtype), size)
    return total


def per_device(
    hidden_in,
    seq_lengths,
    out_grad,
    attn_gain,
    w_query,
    key_matrix,
    value_matrix,
    w_out,
    mlp_gain,
    w_gate,
    w_up,
    w_down,
):
    micro, _, slots, width = hidden_in.shape
    size = lax.axis_size("z")
    z, x, y, c = (lax.axis_index(a) for a in ("z", "x", "y", "c"))
    j = y * 2 + c
    own_rows = w_query.shape[0]
    block_rows = 4 * own_rows
    q_cols = w_query.shape[1] // 4
    kv_cols = key_matrix.shape[1] // 4
    qkv_cols = q_cols + 2 * kv_cols
    ff = w_gate.shape[1]
    chunk = ff // (2 * size)
    rows = micro * slots
    group_rows = 4 * rows
    q_heads = q_cols // HEAD_DIMENSION
    scale = HEAD_DIMENSION ** (-0.5)
    lengths = seq_lengths.reshape(micro)

    def by_head(weight):
        return jnp.swapaxes(weight.reshape(own_rows, 4, -1), 0, 1)

    qkv_local = jnp.concatenate(
        [by_head(w_query), by_head(key_matrix), by_head(value_matrix)], axis=2
    )
    out_local = by_head(w_out)

    def to_heads(local):
        block = jnp.zeros(local.shape, local.dtype)
        for k in range(4):
            piece = pick(local, j ^ k)
            if k:
                piece = lax.ppermute(piece, ("y", "c"), [(i, i ^ k) for i in range(4)])
            block = put(block, piece, j ^ k)
        return block.reshape(block_rows, local.shape[2])

    def whole_zx(block):
        whole = jnp.zeros((size, 2) + block.shape, block.dtype)
        for s, b in enumerate(gather_z(block, size)):
            source = lax.rem(z - s + size, size)
            whole = put(whole, b, source, x)
            whole = put(whole, swap(b, "x"), source, 1 - x)
        return whole.reshape((size * 2 * block.shape[0],) + block.shape[1:])

    tokens = hidden_in.reshape(micro, slots, width)
    token_blocks = gather_yc(tokens)

    gains = jnp.stack([attn_gain, mlp_gain], axis=1).astype(F32)
    gain_blocks = jnp.zeros((4, own_rows, 2), F32)
    for k, g in enumerate(gather_yc(gains)):
        gain_blocks = put(gain_blocks, g, j ^ k)
    gains_all = whole_zx(gain_blocks.reshape(block_rows, 2))
    gain_one, gain_two = gains_all[:, 0][None, :], gains_all[:, 1][None, :]

    wqkv = whole_zx(to_heads(qkv_local))
    wo = whole_zx(to_heads(out_local))

    def to_chunks(local):
        whole = jnp.zeros((size, 2, 2, 2, own_rows, local.shape[2]), local.dtype)
        for s in range(size):
            for k in range(2):
                piece = pick(local, lax.rem(z + s, size) * 2 + (y ^ k), 1)
                if s or k:
                    perm = [
                        (a * 2 + b, ((a + s) % size) * 2 + (b ^ k))
                        for a in range(size)
                        for b in range(2)
                    ]
                    piece = lax.ppermute(piece, ("z", "y"), perm)
                source = lax.rem(z - s + size, size)
                over = swap(piece, "x")
                whole = put(whole, piece, source, x, y ^ k, c)
                whole = put(whole, swap(piece, "c"), source, x, y ^ k, 1 - c)
                whole = put(whole, over, source, 1 - x, y ^ k, c)
                whole = put(whole, swap(over, "c"), source, 1 - x, y ^ k, 1 - c)
        return whole.reshape(width, local.shape[2])

    gate_up_local = jnp.concatenate(
        [w_gate.reshape(own_rows, 2 * size, chunk), w_up.reshape(own_rows, 2 * size, chunk)], axis=2
    )
    wgu = to_chunks(gate_up_local)
    wd = to_chunks(w_down.reshape(own_rows, 2 * size, chunk))

    offsets = jnp.arange(slots, dtype=jnp.int32)
    positions = jnp.concatenate([(j ^ k) * slots + offsets for k in range(4)])
    cosine, sine = rope_tables(positions, HEAD_DIMENSION)
    cosine, sine = cosine[None, :, None, :], sine[None, :, None, :]
    span = 4 * slots
    all_rows = jnp.concatenate(token_blocks, axis=1).astype(F32).reshape(group_rows, width)
    all_scale = lax.rsqrt(jnp.mean(all_rows * all_rows, axis=-1, keepdims=True) + EPS_NORM)
    all_hat = all_rows * all_scale
    xn1 = (all_hat * gain_one).astype(BF)
    qkv = dot(xn1, wqkv)
    q = rotary_embed(
        qkv[:, :q_cols].reshape(micro, span, q_heads, HEAD_DIMENSION), cosine, sine
    ).astype(BF)
    k = rotary_embed(
        qkv[:, q_cols : q_cols + kv_cols].reshape(micro, span, 1, HEAD_DIMENSION), cosine, sine
    ).astype(BF)[:, :, 0]
    v = qkv[:, q_cols + kv_cols :].reshape(micro, span, HEAD_DIMENSION).astype(BF)
    allowed = (positions[None, None, :] <= positions[None, :, None]) & (
        positions[None, None, :] < lengths[:, None, None]
    )
    allowed = allowed[:, None, :, :]
    scores = jnp.einsum("mqgd,msd->mgqs", q, k, preferred_element_type=F32) * scale
    scores = jnp.where(allowed, scores, NEG_FILL)
    top = jnp.max(scores, axis=-1, keepdims=True)
    log_total = top + jnp.log(jnp.sum(jnp.exp(scores - top), axis=-1, keepdims=True))
    probs = jnp.where(allowed, jnp.exp(scores - log_total), 0.0)
    probs_low = probs.astype(BF)
    mixed = (
        jnp.einsum("mgqs,msd->mqgd", probs_low, v, preferred_element_type=F32)
        .astype(BF)
        .reshape(group_rows, q_cols)
    )
    branch_part = dot_right(mixed, wo).astype(BF).reshape(micro, 4, slots, width)
    branch = scatter_yc([branch_part[:, k] for k in range(4)]).reshape(rows, width)

    own_slots = j * slots + offsets
    live = (own_slots[None, :] < lengths[:, None]).astype(F32).reshape(rows, 1)
    own_x = tokens.astype(F32).reshape(rows, width)
    first_scale = lax.rsqrt(jnp.mean(own_x * own_x, axis=-1, keepdims=True) + EPS_NORM)
    first_hat = own_x * first_scale
    middle = own_x + branch
    second_scale = lax.rsqrt(jnp.mean(middle * middle, axis=-1, keepdims=True) + EPS_NORM)
    second_hat = middle * second_scale
    second_normalized = (second_hat * gain_two).astype(BF)
    dy = out_grad.astype(F32).reshape(rows, width) * live

    def joined(block):
        return jnp.concatenate([b for pair in gather_zy(block, size) for b in pair], axis=0)

    dfb = joined(dy.astype(BF))
    xn2 = joined(second_normalized)
    gate_up = dot(xn2, wgu)
    gate, up = gate_up[:, :chunk], gate_up[:, chunk:]
    sigmoid = jax.nn.sigmoid(gate)
    activated = gate * sigmoid
    hidden = (activated * up).astype(BF)
    dhid = dot(dfb, wd)
    dgu = jnp.concatenate(
        [
            (dhid * up * sigmoid * (1.0 + gate * (1.0 - sigmoid))).astype(BF),
            (dhid * activated).astype(BF),
        ],
        axis=1,
    )

    def home(part):
        part = part.astype(BF).reshape(size, 2, rows, width)
        return scatter_z(
            [part[s, 0] for s in range(size)], [part[s, 1] for s in range(size)], "y", size
        )

    dxn2 = home(dot_right(dgu, wgu))
    feed = home(dot_right(hidden, wd))

    def to_owners(grad):
        columns = grad.shape[1]
        grad = grad.astype(BF).reshape(size, 2, 2, 2, own_rows, columns)
        near = pick(grad, c, 3).astype(F32) + swap(pick(grad, 1 - c, 3), "c")
        near = near.astype(BF)
        total = (pick(near, x, 1).astype(F32) + swap(pick(near, 1 - x, 1), "x")).astype(BF)
        result = jnp.zeros((2 * size, own_rows, columns), BF)
        for s in range(size):
            for k in range(2):
                piece = pick(pick(total, lax.rem(z + s, size)), y ^ k)
                if s or k:
                    perm = [
                        (a * 2 + b, ((a + s) % size) * 2 + (b ^ k))
                        for a in range(size)
                        for b in range(2)
                    ]
                    piece = lax.ppermute(piece, ("z", "y"), perm)
                result = put(result, piece, lax.rem(z - s + size, size) * 2 + (y ^ k))
        return jnp.swapaxes(result, 0, 1).astype(F32)

    gate_up_grad = to_owners(dot_rows(xn2, dgu))
    grad_gate = gate_up_grad[:, :, :chunk].reshape(own_rows, ff)
    grad_up = gate_up_grad[:, :, chunk:].reshape(own_rows, ff)
    grad_down = to_owners(dot_rows(dfb, hidden)).reshape(own_rows, ff)

    outputs = (live * (middle + feed)).astype(BF).reshape(hidden_in.shape)

    gain_two_part = jnp.sum(second_hat * dxn2, axis=0)
    dh1 = dy + norm_backward(second_hat, second_scale, dxn2 * gain_two)
    dab = jnp.concatenate(gather_yc(dh1.astype(BF).reshape(micro, slots, width)), axis=1).reshape(
        group_rows, width
    )
    dob = dot(dab, wo).astype(BF).reshape(micro, span, q_heads, HEAD_DIMENSION)
    dprob = jnp.einsum("mqgd,msd->mgqs", dob, v, preferred_element_type=F32)
    dscore = (probs * (dprob - jnp.sum(probs * dprob, axis=-1, keepdims=True))).astype(BF)
    dq = jnp.einsum("mgqs,msd->mqgd", dscore, k, preferred_element_type=F32) * scale
    dk = jnp.einsum("mgqs,mqgd->msd", dscore, q, preferred_element_type=F32) * scale
    dv = jnp.einsum("mgqs,mqgd->msd", probs_low, dob, preferred_element_type=F32)
    dq = rotary_backward(dq, cosine, sine).astype(BF).reshape(group_rows, q_cols)
    dk = rotary_backward(dk[:, :, None, :], cosine, sine).astype(BF).reshape(group_rows, kv_cols)
    dqkv = jnp.concatenate([dq, dk, dv.astype(BF).reshape(group_rows, kv_cols)], axis=1)
    dxn1_part = dot_right(dqkv, wqkv)
    gain_one_part = jnp.sum(all_hat * dxn1_part, axis=0)

    def to_blocks(grad):
        grad = grad.reshape((size, 2, block_rows) + grad.shape[1:])
        parts, partners = [], []
        for s in range(size):
            at = pick(grad, lax.rem(z - s + size, size))
            parts.append(pick(at, x))
            partners.append(pick(at, 1 - x))
        return scatter_z(parts, partners, "x", size)

    def to_rows(block):
        block = block.astype(BF).reshape(4, own_rows, -1)
        result = jnp.zeros(block.shape, BF)
        for k in range(4):
            piece = pick(block, j ^ k)
            if k:
                piece = lax.ppermute(piece, ("y", "c"), [(i, i ^ k) for i in range(4)])
            result = put(result, piece, j ^ k)
        return jnp.swapaxes(result, 0, 1).astype(F32)

    out_grads = to_rows(to_blocks(dot_rows(dab, mixed).astype(BF)))
    qkv_grads = to_rows(to_blocks(dot_rows(xn1, dqkv).astype(BF)))
    grad_query = qkv_grads[:, :, :q_cols].reshape(own_rows, 4 * q_cols)
    grad_key = qkv_grads[:, :, q_cols : q_cols + kv_cols].reshape(own_rows, 4 * kv_cols)
    grad_value = qkv_grads[:, :, q_cols + kv_cols :].reshape(own_rows, 4 * kv_cols)
    grad_out = out_grads.reshape(own_rows, 4 * q_cols)

    gain_block = to_blocks(jnp.stack([gain_one_part, gain_two_part], axis=1))
    gain_block = gain_block.reshape(4, own_rows, 2)
    gain_grads = pick(gain_block, j)
    for k in range(1, 4):
        gain_grads = gain_grads + lax.ppermute(
            pick(gain_block, j ^ k), ("y", "c"), [(i, i ^ k) for i in range(4)]
        )

    dxn1_part = dxn1_part.astype(BF).reshape(micro, 4, slots, width)
    dxn1 = scatter_yc([dxn1_part[:, k] for k in range(4)]).reshape(rows, width)
    input_grads = (
        (dh1 + norm_backward(first_hat, first_scale, dxn1 * gain_one))
        .astype(BF)
        .reshape(hidden_in.shape)
    )
    return (
        outputs,
        input_grads,
        gain_grads[:, 0],
        grad_query,
        grad_key,
        grad_value,
        grad_out,
        gain_grads[:, 1],
        grad_gate,
        grad_up,
        grad_down,
    )


def solution(mesh):
    dp, fsdp = mesh.shape["dp"], mesh.shape["fsdp"]
    fine = Mesh(mesh.devices.reshape(dp // 2, 2, fsdp // 2, 2), ("z", "x", "y", "c"))
    batch, slot, both = ("z", "x"), ("y", "c"), ("z", "x", "y", "c")
    vector, matrix = P(both), P(both, None)
    rows = P(None, batch, slot, None)
    return jax.shard_map(
        per_device,
        mesh=fine,
        in_specs=(rows, P(None, batch), rows) + (vector,) + (matrix,) * 4 + (vector,) + (matrix,) * 3,
        out_specs=(rows, rows, vector) + (matrix,) * 4 + (vector,) + (matrix,) * 3,
        check_vma=False,
    )
```

```python
import jax
import jax.numpy as jnp
from jax import lax
from jax.sharding import Mesh, PartitionSpec as P

QUERY_HEADS = 8
KEY_VALUE_HEADS = 4
HEAD_DIMENSION = 256

EPS_NORM = 1e-06
ROPE_BASE = 1000042.0
NEG_FILL = -1e30

BF = jnp.bfloat16
F32 = jnp.float32


def rope_tables(positions, head_size):
    half_size = head_size // 2
    inverse = ROPE_BASE ** (-(jnp.arange(half_size, dtype=F32) * 2.0 / head_size))
    angles = positions.astype(F32)[:, None] * inverse[None, :]
    return jnp.cos(angles), jnp.sin(angles)


def rotary_embed(rows, cosine, sine):
    half = rows.shape[-1] // 2
    first, second = rows[..., :half], rows[..., half:]
    return jnp.concatenate(
        [first * cosine - second * sine, second * cosine + first * sine], axis=-1
    )


def rotary_backward(grads, cosine, sine):
    half = grads.shape[-1] // 2
    first, second = grads[..., :half], grads[..., half:]
    return jnp.concatenate(
        [first * cosine + second * sine, second * cosine - first * sine], axis=-1
    )


def norm_backward(normalized, reciprocal, gradient):
    return reciprocal * (
        gradient - normalized * jnp.mean(gradient * normalized, axis=-1, keepdims=True)
    )


def dot(left, right):
    return jnp.dot(left, right, preferred_element_type=F32)


def dot_right(left, right):
    return lax.dot_general(left, right, (((1,), (1,)), ((), ())), preferred_element_type=F32)


def dot_rows(left, right):
    return lax.dot_general(left, right, (((0,), (0,)), ((), ())), preferred_element_type=F32)


def swap(value, axis):
    return lax.ppermute(value, axis, [(0, 1), (1, 0)])


def ring(value, size):
    return lax.ppermute(value, "z", [(i, (i + 1) % size) for i in range(size)])


def pick(value, index, axis=0):
    return lax.dynamic_index_in_dim(value, index, axis, keepdims=False)


def put(buffer, piece, *index):
    piece = piece.reshape((1,) * len(index) + piece.shape)
    starts = tuple(index) + (0,) * (buffer.ndim - len(index))
    return lax.dynamic_update_slice(buffer, piece, starts)


def tie(*values):
    return lax.optimization_barrier(values)


def cut(value, start, count, axis):
    return lax.dynamic_slice_in_dim(value, start, count, axis)


def swap_cores(blocks):
    return [[swap(b[i], "c") for i in range(b.shape[0])] for b in blocks]


def gather_yc(block, across=None):
    if across is None:
        across = swap(block, "y")
    near, far = (jnp.stack(b) for b in swap_cores([block, across]))
    return [block, near, across, far]


def scatter_yc(parts):
    far, near = (jnp.stack(b) for b in swap_cores([parts[3], parts[1]]))
    away = (parts[2].astype(F32) + far).astype(BF)
    return parts[0].astype(F32) + near + swap(away, "y")


def to_peers_yc(piece_for):
    pieces = [piece_for(0)]
    for k in range(1, 4):
        pieces.append(lax.ppermute(piece_for(k), ("y", "c"), [(i, i ^ k) for i in range(4)]))
    return pieces


def swap_in_turn(pieces, axis):
    got = []
    for piece in pieces:
        if got:
            piece, got[-1] = tie(piece, got[-1])
        got.append(swap(piece, axis))
    return got


def scatter_z(parts, partners, axis, size, ties=None):
    total = None
    order = [(step + 1) % size for step in range(size)]
    got = swap_in_turn([partners[s] for s in order], axis)
    for step in range(size):
        own = parts[order[step]].astype(F32) + got[step]
        total = own if total is None else own + ring(total, size)
        if step < size - 1:
            total = total.astype(BF)
            if ties and step in ties:
                total, *ties[step] = tie(total, *ties[step])
    return total


def per_device(
    hidden_in,
    seq_lengths,
    out_grad,
    attn_gain,
    w_query,
    key_matrix,
    value_matrix,
    w_out,
    mlp_gain,
    w_gate,
    w_up,
    w_down,
):
    micro, _, slots, width = hidden_in.shape
    size = lax.axis_size("z")
    z, x, y, c = (lax.axis_index(a) for a in ("z", "x", "y", "c"))
    j = y * 2 + c
    own_rows = w_query.shape[0]
    block_rows = 4 * own_rows
    q_cols = w_query.shape[1] // 4
    kv_cols = key_matrix.shape[1] // 4
    qkv_cols = q_cols + 2 * kv_cols
    ff = w_gate.shape[1]
    chunk = ff // (2 * size)
    rows = micro * slots
    group_rows = 4 * rows
    span = 4 * slots
    q_heads = q_cols // HEAD_DIMENSION
    scale = HEAD_DIMENSION ** (-0.5)
    lengths = seq_lengths.reshape(micro)

    def behind(s):
        return lax.rem(z - s + size, size)

    def by_chunk(weight):
        return jnp.swapaxes(weight.reshape(own_rows, 2 * size, chunk), 0, 1)

    def exchange(parts):
        return lax.all_to_all(parts, ("z", "y"), 0, 0, tiled=True)

    offsets = jnp.arange(slots, dtype=jnp.int32)
    own_slots = j * slots + offsets
    live = (own_slots[None, :] < lengths[:, None]).astype(F32).reshape(rows, 1)
    dy = out_grad.astype(F32).reshape(rows, width) * live
    dfb_around = [dy.astype(BF)]
    dfb_around.append(ring(dfb_around[-1], size))

    def beside(values, columns):
        return jnp.pad(values, ((0, 8 - values.shape[0]), (0, columns - values.shape[1])))

    gains = jnp.stack([attn_gain, mlp_gain])

    def head_piece(k):
        to = j ^ k
        weights = jnp.concatenate(
            [
                cut(w_query, to * q_cols, q_cols, 1),
                cut(key_matrix, to * kv_cols, kv_cols, 1),
                cut(value_matrix, to * kv_cols, kv_cols, 1),
                cut(w_out, to * q_cols, q_cols, 1),
            ],
            axis=1,
        )
        return jnp.concatenate([weights, beside(gains, weights.shape[1])], axis=0)

    head_pieces = to_peers_yc(head_piece)

    head_cols = qkv_cols + q_cols
    block = jnp.zeros((4, own_rows, head_cols), BF)
    gain_block = jnp.zeros((4, 2, own_rows), BF)
    for k, piece in enumerate(head_pieces):
        block = put(block, piece[:own_rows], j ^ k)
        gain_block = put(gain_block, piece[own_rows : own_rows + 2, :own_rows], j ^ k)
    gain_block = jnp.swapaxes(gain_block, 0, 1).reshape(2, block_rows)
    block = jnp.concatenate(
        [block.reshape(block_rows, head_cols), beside(gain_block, head_cols)], axis=0
    )

    block, dfb_around[1], hidden_in, w_gate, w_up, w_down = tie(
        block, dfb_around[1], hidden_in, w_gate, w_up, w_down
    )
    tokens = hidden_in.reshape(micro, slots, width)
    around, over = [block], []
    across = [swap(tokens, "y")]
    token_blocks = gather_yc(tokens, across[0])
    for s in range(1, size):
        over.append(swap(around[-1], "x"))
        around.append(ring(around[-1], size))
        around[s], over[s - 1] = tie(around[s], over[s - 1])
        if s < size - 1:
            dfb_around.append(ring(dfb_around[-1], size))
            around[s], dfb_around[s + 1] = tie(around[s], dfb_around[s + 1])
        if s == size - 2:
            around[s], *token_blocks = tie(around[s], *token_blocks)
    dfb_over = swap_in_turn(dfb_around, "y")
    gate_up_local = jnp.concatenate([by_chunk(w_gate), by_chunk(w_up)], axis=2)
    gate_up_local, around[-1], *dfb_over = tie(gate_up_local, around[-1], *dfb_over)
    gate_up_mine = exchange(gate_up_local)
    over.append(swap(around[-1], "x"))
    down_local, gate_up_mine = tie(by_chunk(w_down), gate_up_mine)
    down_mine = exchange(down_local)
    gate_up_over = swap(gate_up_mine, "x")

    wqkv = jnp.zeros((size, 2, block_rows, qkv_cols), BF)
    gains_all = jnp.zeros((size, 2, 2, block_rows), BF)
    wo = jnp.zeros((size, 2, block_rows, q_cols), BF)
    for s in range(size):
        for at, piece in ((x, around[s]), (1 - x, over[s])):
            wqkv = put(wqkv, piece[:block_rows, :qkv_cols], behind(s), at)
            wo = put(wo, piece[:block_rows, qkv_cols:], behind(s), at)
            gains_all = put(gains_all, piece[block_rows : block_rows + 2, :block_rows], behind(s), at)
    wqkv = wqkv.reshape(width, qkv_cols)
    wo = wo.reshape(width, q_cols)
    gain_one = gains_all[:, :, 0].astype(F32).reshape(1, width)
    gain_two = gains_all[:, :, 1].astype(F32).reshape(1, width)

    def put_rows(whole, piece, at):
        piece = piece.reshape(size, 1, 2, 1, own_rows, piece.shape[2])
        whole = lax.dynamic_update_slice(whole, piece, (0, at, 0, c, 0, 0))
        for i in range(0, size, size // 4):
            part = swap(piece[i : i + size // 4], "c")
            whole = lax.dynamic_update_slice(whole, part, (i, at, 0, 1 - c, 0, 0))
        return whole

    def empty_rows(columns):
        return jnp.zeros((size, 2, 2, 2, own_rows, columns), BF)

    positions = jnp.concatenate([(j ^ k) * slots + offsets for k in range(4)])
    cosine, sine = rope_tables(positions, HEAD_DIMENSION)
    cosine, sine = cosine[None, :, None, :], sine[None, :, None, :]
    all_x = jnp.concatenate(token_blocks, axis=1).astype(F32).reshape(group_rows, width)
    all_scale = lax.rsqrt(jnp.mean(all_x * all_x, axis=-1, keepdims=True) + EPS_NORM)
    xn1 = (all_x * all_scale * gain_one).astype(BF)
    qkv = dot(xn1, wqkv)
    q = rotary_embed(
        qkv[:, :q_cols].reshape(micro, span, q_heads, HEAD_DIMENSION), cosine, sine
    ).astype(BF)
    k = rotary_embed(
        qkv[:, q_cols : q_cols + kv_cols].reshape(micro, span, 1, HEAD_DIMENSION), cosine, sine
    ).astype(BF)[:, :, 0]
    v = qkv[:, q_cols + kv_cols :].reshape(micro, span, HEAD_DIMENSION).astype(BF)
    allowed = (positions[None, None, :] <= positions[None, :, None]) & (
        positions[None, None, :] < lengths[:, None, None]
    )
    allowed = allowed[:, None, :, :]
    scores = jnp.einsum("mqgd,msd->mgqs", q, k, preferred_element_type=F32) * scale
    scores = jnp.where(allowed, scores, NEG_FILL)
    top = jnp.max(scores, axis=-1, keepdims=True)
    log_total = top + jnp.log(jnp.sum(jnp.exp(scores - top), axis=-1, keepdims=True))
    probs = jnp.where(allowed, jnp.exp(scores - log_total), 0.0)
    probs_low = probs.astype(BF)
    mixed = (
        jnp.einsum("mgqs,msd->mqgd", probs_low, v, preferred_element_type=F32)
        .astype(BF)
        .reshape(group_rows, q_cols)
    )
    branch_part = dot_right(mixed, wo).astype(BF).reshape(micro, 4, slots, width)
    branch = scatter_yc([branch_part[:, i] for i in range(4)]).reshape(rows, width)

    own_x = tokens.astype(F32).reshape(rows, width)
    first_scale = lax.rsqrt(jnp.mean(own_x * own_x, axis=-1, keepdims=True) + EPS_NORM)
    first_hat = own_x * first_scale
    middle = own_x + branch
    second_scale = lax.rsqrt(jnp.mean(middle * middle, axis=-1, keepdims=True) + EPS_NORM)
    second_hat = middle * second_scale
    second_normalized = (second_hat * gain_two).astype(BF)

    second_normalized, down_mine = tie(second_normalized, down_mine)
    xn2_around = [second_normalized, ring(second_normalized, size)]
    down_mine, gate_up_over = tie(down_mine, gate_up_over)
    down_over = swap(down_mine, "x")
    wgu = put_rows(put_rows(empty_rows(2 * chunk), gate_up_mine, x), gate_up_over, 1 - x)
    wd = put_rows(put_rows(empty_rows(chunk), down_mine, x), down_over, 1 - x)
    for s in range(2, size):
        come = ring(xn2_around[-1], size)
        xn2_around.append(come)
    wgu = wgu.reshape(width, 2 * chunk)
    wd = wd.reshape(width, chunk)
    xn2_blocks = [b for near in xn2_around for b in (near, swap(near, "y"))]
    dfb_blocks = [b for pair in zip(dfb_around, dfb_over) for b in pair]

    halves = []
    for part in (slice(0, -2), slice(-2, None)):
        xn2 = jnp.concatenate(xn2_blocks[part], axis=0)
        dfb = jnp.concatenate(dfb_blocks[part], axis=0)
        if halves:
            xn2, *halves[0] = tie(xn2, *halves[0])
        gate_up = dot(xn2, wgu)
        gate, up = gate_up[:, :chunk], gate_up[:, chunk:]
        sigmoid = jax.nn.sigmoid(gate)
        activated = gate * sigmoid
        hidden = (activated * up).astype(BF)
        dhid = dot(dfb, wd)
        dgu = jnp.concatenate(
            [
                (dhid * up * sigmoid * (1.0 + gate * (1.0 - sigmoid))).astype(BF),
                (dhid * activated).astype(BF),
            ],
            axis=1,
        )
        if halves:
            ahead = halves[0][4].reshape(size - 1, 2, rows, width)[1]
            first_total = (ahead[0].astype(F32) + swap(ahead[1], "y")).astype(BF)
            first_total, dgu = tie(first_total, dgu)
        dxn2_part = dot_right(dgu, wgu).astype(BF)
        halves.append([xn2, dfb, hidden, dgu, dxn2_part])

    def pieces(parts):
        parts = [p.reshape(-1, 2, rows, width) for p in parts]
        return [[p[s, i] for p in parts for s in range(p.shape[0])] for i in range(2)]

    def over_cores(grad, pieces):
        grad = grad.reshape(size, 2, 2, 2, own_rows, grad.shape[1])
        sums = []
        for i in range(0, size, size // pieces):
            part = grad[i : i + size // pieces]
            sums.append((pick(part, c, 3).astype(F32) + swap(pick(part, 1 - c, 3), "c")).astype(BF))
        return jnp.concatenate(sums, axis=0)

    def over_x(grad):
        total = (pick(grad, x, 1).astype(F32) + swap(pick(grad, 1 - x, 1), "x")).astype(BF)
        return total.reshape(2 * size, own_rows, grad.shape[-1])

    (xn2_a, dfb_a, hidden_a, dgu_a, dxn2_a), (xn2_b, dfb_b, hidden_b, dgu_b, dxn2_b) = halves
    own, away = pieces([dxn2_a, dxn2_b])
    order = [(step + 1) % size for step in range(1, size)]
    away[order[0]], first_total = tie(away[order[0]], first_total)
    got = swap_in_turn([away[s] for s in order], "y")
    dxn2_b, hidden_b, dfb_a, xn2_a = tie(dxn2_b, hidden_b, dfb_a, xn2_a)
    down_grad = (dot_rows(dfb_a, hidden_a) + dot_rows(dfb_b, hidden_b)).astype(BF)
    total = first_total
    for step in range(1, size):
        total = own[order[step - 1]].astype(F32) + got[step - 1] + ring(total, size)
        if step < size - 1:
            total = total.astype(BF)
        if step == 1:
            total, down_grad, xn2_a = tie(total, down_grad, xn2_a)
            down_near = over_cores(down_grad, 2)
            gate_up_grad = dot_rows(xn2_a, dgu_a)
        if step == size - 2:
            total, gate_up_grad = tie(total, gate_up_grad)
            gate_up_grad = (gate_up_grad + dot_rows(xn2_b, dgu_b)).astype(BF)
    feed_a, feed_b = dot_right(hidden_a, wd).astype(BF), dot_right(hidden_b, wd).astype(BF)
    down_sum = over_x(down_near)
    dxn2, gate_up_grad, feed_a, feed_b = tie(total, gate_up_grad, feed_a, feed_b)
    gate_up_sum = over_x(over_cores(gate_up_grad, 4))

    dh1 = dy + norm_backward(second_hat, second_scale, dxn2 * gain_two)
    dab_blocks = gather_yc(dh1.astype(BF).reshape(micro, slots, width))
    dab_blocks[2], down_sum = tie(dab_blocks[2], down_sum)
    down_parts = exchange(down_sum)
    dab_blocks[3], feed_a, feed_b = tie(dab_blocks[3], feed_a, feed_b)
    dab = jnp.concatenate(dab_blocks, axis=1).reshape(group_rows, width)

    def blocks_of(*grads):
        grads = [g.reshape(size, 2, block_rows, g.shape[1]) for g in grads]
        at = [[pick(g, behind(s)) for g in grads] for s in range(size)]
        return [
            [jnp.concatenate([pick(g, i) for g in gs], axis=1) for gs in at] for i in (x, 1 - x)
        ]

    out_grad_part = dot_rows(dab, mixed).astype(BF)

    dob = dot(dab, wo).astype(BF)
    dob = dob.reshape(micro, span, q_heads, HEAD_DIMENSION)
    dprob = jnp.einsum("mqgd,msd->mgqs", dob, v, preferred_element_type=F32)
    dscore = (probs * (dprob - jnp.sum(probs * dprob, axis=-1, keepdims=True))).astype(BF)
    dq = jnp.einsum("mgqs,msd->mqgd", dscore, k, preferred_element_type=F32) * scale
    dk = jnp.einsum("mgqs,mqgd->msd", dscore, q, preferred_element_type=F32) * scale
    dv = jnp.einsum("mgqs,mqgd->msd", probs_low, dob, preferred_element_type=F32)
    dq = rotary_backward(dq, cosine, sine).astype(BF).reshape(group_rows, q_cols)
    dk = rotary_backward(dk[:, :, None, :], cosine, sine).astype(BF).reshape(group_rows, kv_cols)
    dqkv = jnp.concatenate([dq, dk, dv.astype(BF).reshape(group_rows, kv_cols)], axis=1)

    dqkv, gate_up_sum = tie(dqkv, gate_up_sum)
    gate_up_parts = exchange(gate_up_sum)
    feed = scatter_z(*pieces([feed_a, feed_b]), "y", size)
    outputs = (live * (middle + feed)).astype(BF)
    head_ties = {size - 2: [outputs]}
    head_sum = scatter_z(
        *blocks_of(dot_rows(xn1, dqkv).astype(BF), out_grad_part), "x", size, head_ties
    )
    (outputs,) = head_ties[size - 2]
    outputs = outputs.reshape(hidden_in.shape)

    dxn1_part = dot_right(dqkv, wqkv).astype(BF).reshape(micro, 4, slots, width)
    dxn1 = scatter_yc([dxn1_part[:, i] for i in range(4)]).reshape(rows, width)
    input_grads = (
        (dh1 + norm_backward(first_hat, first_scale, dxn1 * gain_one))
        .astype(BF)
        .reshape(hidden_in.shape)
    )

    def owned(block):
        block = block.astype(BF)
        came = to_peers_yc(lambda k: cut(block, (j ^ k) * own_rows, own_rows, 0))
        heads = jnp.zeros((4, own_rows, block.shape[1]), BF)
        for k in range(4):
            heads = put(heads, came[k], j ^ k)
        return heads

    def side_by_side(parts, start, count):
        return jnp.concatenate(
            [parts[i, :, start : start + count] for i in range(parts.shape[0])], axis=1
        ).astype(F32)

    heads = owned(head_sum)
    grad_query = side_by_side(heads, 0, q_cols)
    grad_key = side_by_side(heads, q_cols, kv_cols)
    grad_value = side_by_side(heads, q_cols + kv_cols, kv_cols)
    grad_out = side_by_side(heads, qkv_cols, q_cols)
    grad_gate = side_by_side(gate_up_parts, 0, chunk)
    grad_up = side_by_side(gate_up_parts, chunk, chunk)
    grad_down = side_by_side(down_parts, 0, chunk)

    def gain_gradient(gain, *pairs):
        total = sum(jnp.sum(w.astype(F32) * g, axis=1) for w, g in pairs)
        return total / gain.astype(F32)

    grad_attn_gain = gain_gradient(
        attn_gain, (w_query, grad_query), (key_matrix, grad_key), (value_matrix, grad_value)
    )
    grad_mlp_gain = gain_gradient(mlp_gain, (w_gate, grad_gate), (w_up, grad_up))
    return (
        outputs,
        input_grads,
        grad_attn_gain,
        grad_query,
        grad_key,
        grad_value,
        grad_out,
        grad_mlp_gain,
        grad_gate,
        grad_up,
        grad_down,
    )


def solution(mesh):
    dp, fsdp = mesh.shape["dp"], mesh.shape["fsdp"]
    fine = Mesh(mesh.devices.reshape(dp // 2, 2, fsdp // 2, 2), ("z", "x", "y", "c"))
    batch, slot, both = ("z", "x"), ("y", "c"), ("z", "x", "y", "c")
    vector, matrix = P(both), P(both, None)
    rows = P(None, batch, slot, None)
    return jax.shard_map(
        per_device,
        mesh=fine,
        in_specs=(rows, P(None, batch), rows) + (vector,) + (matrix,) * 4 + (vector,) + (matrix,) * 3,
        out_specs=(rows, rows, vector) + (matrix,) * 4 + (vector,) + (matrix,) * 3,
        check_vma=False,
    )
```

```python
import jax
import jax.numpy as jnp
from jax import lax
from jax.sharding import Mesh, PartitionSpec as P

QUERY_HEADS = 8
KEY_VALUE_HEADS = 4
HEAD_DIMENSION = 256

EPS_NORM = 1e-06
ROPE_BASE = 1000042.0
NEG_FILL = -1e30

BF = jnp.bfloat16
F32 = jnp.float32


def rope_tables(positions, head_size):
    half_size = head_size // 2
    inverse = ROPE_BASE ** (-(jnp.arange(half_size, dtype=F32) * 2.0 / head_size))
    angles = positions.astype(F32)[:, None] * inverse[None, :]
    return jnp.cos(angles), jnp.sin(angles)


def rotary_embed(rows, cosine, sine):
    half = rows.shape[-1] // 2
    first, second = rows[..., :half], rows[..., half:]
    return jnp.concatenate(
        [first * cosine - second * sine, second * cosine + first * sine], axis=-1
    )


def rotary_backward(grads, cosine, sine):
    half = grads.shape[-1] // 2
    first, second = grads[..., :half], grads[..., half:]
    return jnp.concatenate(
        [first * cosine + second * sine, second * cosine - first * sine], axis=-1
    )


def norm_backward(normalized, reciprocal, gradient):
    return reciprocal * (
        gradient - normalized * jnp.mean(gradient * normalized, axis=-1, keepdims=True)
    )


def dot(left, right):
    return jnp.dot(left, right, preferred_element_type=F32)


def dot_right(left, right):
    return lax.dot_general(left, right, (((1,), (1,)), ((), ())), preferred_element_type=F32)


def dot_rows(left, right):
    return lax.dot_general(left, right, (((0,), (0,)), ((), ())), preferred_element_type=F32)


def swap(value, axis):
    return lax.ppermute(value, axis, [(0, 1), (1, 0)])


def ring(value, size):
    return lax.ppermute(value, "z", [(i, (i + 1) % size) for i in range(size)])


def pick(value, index, axis=0):
    return lax.dynamic_index_in_dim(value, index, axis, keepdims=False)


def put(buffer, piece, *index):
    piece = piece.reshape((1,) * len(index) + piece.shape)
    starts = tuple(index) + (0,) * (buffer.ndim - len(index))
    return lax.dynamic_update_slice(buffer, piece, starts)


def tie(*values):
    return lax.optimization_barrier(values)


def cut(value, start, count, axis):
    return lax.dynamic_slice_in_dim(value, start, count, axis)


def swap_cores(blocks):
    return [[swap(b[i], "c") for i in range(b.shape[0])] for b in blocks]


def gather_yc(block, across=None):
    if across is None:
        across = swap(block, "y")
    near, far = (jnp.stack(b) for b in swap_cores([block, across]))
    return [block, near, across, far]


def scatter_yc(parts):
    far, near = (jnp.stack(b) for b in swap_cores([parts[3], parts[1]]))
    away = (parts[2].astype(F32) + far).astype(BF)
    return parts[0].astype(F32) + near + swap(away, "y")


def to_peers_yc(piece_for):
    pieces = [piece_for(0)]
    for k in range(1, 4):
        pieces.append(lax.ppermute(piece_for(k), ("y", "c"), [(i, i ^ k) for i in range(4)]))
    return pieces


def swap_in_turn(pieces, axis):
    got = []
    for piece in pieces:
        if got:
            piece, got[-1] = tie(piece, got[-1])
        got.append(swap(piece, axis))
    return got


def scatter_z(parts, partners, axis, size, ties=None):
    total = None
    order = [(step + 1) % size for step in range(size)]
    got = swap_in_turn([partners[s] for s in order], axis)
    for step in range(size):
        own = parts[order[step]].astype(F32) + got[step]
        total = own if total is None else own + ring(total, size)
        if step < size - 1:
            total = total.astype(BF)
            if ties and step in ties:
                total, *ties[step] = tie(total, *ties[step])
    return total


def per_device(
    hidden_in,
    seq_lengths,
    out_grad,
    attn_gain,
    w_query,
    key_matrix,
    value_matrix,
    w_out,
    mlp_gain,
    w_gate,
    w_up,
    w_down,
):
    micro, _, slots, width = hidden_in.shape
    size = lax.axis_size("z")
    z, x, y, c = (lax.axis_index(a) for a in ("z", "x", "y", "c"))
    j = y * 2 + c
    own_rows = w_query.shape[0]
    block_rows = 4 * own_rows
    q_cols = w_query.shape[1] // 4
    kv_cols = key_matrix.shape[1] // 4
    qkv_cols = q_cols + 2 * kv_cols
    ff = w_gate.shape[1]
    chunk = ff // (2 * size)
    rows = micro * slots
    group_rows = 4 * rows
    span = 4 * slots
    q_heads = q_cols // HEAD_DIMENSION
    scale = HEAD_DIMENSION ** (-0.5)
    lengths = seq_lengths.reshape(micro)

    def behind(s):
        return lax.rem(z - s + size, size)

    def by_chunk(weight):
        return jnp.swapaxes(weight.reshape(own_rows, 2 * size, chunk), 0, 1)

    def exchange(parts):
        return lax.all_to_all(parts, ("z", "y"), 0, 0, tiled=True)

    offsets = jnp.arange(slots, dtype=jnp.int32)
    own_slots = j * slots + offsets
    live = (own_slots[None, :] < lengths[:, None]).astype(F32).reshape(rows, 1)
    dy = out_grad.astype(F32).reshape(rows, width) * live
    dfb_around = [dy.astype(BF)]
    dfb_around.append(ring(dfb_around[-1], size))

    def beside(values, columns):
        return jnp.pad(values, ((0, 8 - values.shape[0]), (0, columns - values.shape[1])))

    gains = jnp.stack([attn_gain, mlp_gain])

    def head_piece(k):
        to = j ^ k
        weights = jnp.concatenate(
            [
                cut(w_query, to * q_cols, q_cols, 1),
                cut(key_matrix, to * kv_cols, kv_cols, 1),
                cut(value_matrix, to * kv_cols, kv_cols, 1),
                cut(w_out, to * q_cols, q_cols, 1),
            ],
            axis=1,
        )
        return jnp.concatenate([weights, beside(gains, weights.shape[1])], axis=0)

    head_pieces = to_peers_yc(head_piece)

    head_cols = qkv_cols + q_cols
    block = jnp.zeros((4, own_rows, head_cols), BF)
    gain_block = jnp.zeros((4, 2, own_rows), BF)
    for k, piece in enumerate(head_pieces):
        block = put(block, piece[:own_rows], j ^ k)
        gain_block = put(gain_block, piece[own_rows : own_rows + 2, :own_rows], j ^ k)
    gain_block = jnp.swapaxes(gain_block, 0, 1).reshape(2, block_rows)
    block = jnp.concatenate(
        [block.reshape(block_rows, head_cols), beside(gain_block, head_cols)], axis=0
    )

    block, dfb_around[1], hidden_in, w_gate, w_up, w_down = tie(
        block, dfb_around[1], hidden_in, w_gate, w_up, w_down
    )
    tokens = hidden_in.reshape(micro, slots, width)
    around, over = [block], []
    across = [swap(tokens, "y")]
    token_blocks = gather_yc(tokens, across[0])
    for s in range(1, size):
        over.append(swap(around[-1], "x"))
        around.append(ring(around[-1], size))
        around[s], over[s - 1] = tie(around[s], over[s - 1])
        if s < size - 1:
            dfb_around.append(ring(dfb_around[-1], size))
            around[s], dfb_around[s + 1] = tie(around[s], dfb_around[s + 1])
        if s == size - 2:
            around[s], *token_blocks = tie(around[s], *token_blocks)
    dfb_over = swap_in_turn(dfb_around, "y")
    gate_up_local = jnp.concatenate([by_chunk(w_gate), by_chunk(w_up)], axis=2)
    gate_up_local, around[-1], *dfb_over = tie(gate_up_local, around[-1], *dfb_over)
    gate_up_mine = exchange(gate_up_local)
    over.append(swap(around[-1], "x"))
    gate_up_over = swap(gate_up_mine, "x")

    wqkv = jnp.zeros((size, 2, block_rows, qkv_cols), BF)
    gains_all = jnp.zeros((size, 2, 2, block_rows), BF)
    wo = jnp.zeros((size, 2, block_rows, q_cols), BF)
    for s in range(size):
        for at, piece in ((x, around[s]), (1 - x, over[s])):
            wqkv = put(wqkv, piece[:block_rows, :qkv_cols], behind(s), at)
            wo = put(wo, piece[:block_rows, qkv_cols:], behind(s), at)
            gains_all = put(gains_all, piece[block_rows : block_rows + 2, :block_rows], behind(s), at)
    wqkv = wqkv.reshape(width, qkv_cols)
    wo = wo.reshape(width, q_cols)
    gain_one = gains_all[:, :, 0].astype(F32).reshape(1, width)
    gain_two = gains_all[:, :, 1].astype(F32).reshape(1, width)

    def put_rows(whole, piece, at):
        piece = piece.reshape(size, 1, 2, 1, own_rows, piece.shape[2])
        whole = lax.dynamic_update_slice(whole, piece, (0, at, 0, c, 0, 0))
        for i in range(0, size, size // 4):
            part = swap(piece[i : i + size // 4], "c")
            whole = lax.dynamic_update_slice(whole, part, (i, at, 0, 1 - c, 0, 0))
        return whole

    def empty_rows(columns):
        return jnp.zeros((size, 2, 2, 2, own_rows, columns), BF)

    positions = jnp.concatenate([(j ^ k) * slots + offsets for k in range(4)])
    cosine, sine = rope_tables(positions, HEAD_DIMENSION)
    cosine, sine = cosine[None, :, None, :], sine[None, :, None, :]
    all_x = jnp.concatenate(token_blocks, axis=1).astype(F32).reshape(group_rows, width)
    all_scale = lax.rsqrt(jnp.mean(all_x * all_x, axis=-1, keepdims=True) + EPS_NORM)
    xn1 = (all_x * all_scale * gain_one).astype(BF)
    qkv = dot(xn1, wqkv)
    q = rotary_embed(
        qkv[:, :q_cols].reshape(micro, span, q_heads, HEAD_DIMENSION), cosine, sine
    ).astype(BF)
    k = rotary_embed(
        qkv[:, q_cols : q_cols + kv_cols].reshape(micro, span, 1, HEAD_DIMENSION), cosine, sine
    ).astype(BF)[:, :, 0]
    v = qkv[:, q_cols + kv_cols :].reshape(micro, span, HEAD_DIMENSION).astype(BF)
    allowed = (positions[None, None, :] <= positions[None, :, None]) & (
        positions[None, None, :] < lengths[:, None, None]
    )
    allowed = allowed[:, None, :, :]
    scores = jnp.einsum("mqgd,msd->mgqs", q, k, preferred_element_type=F32) * scale
    scores = jnp.where(allowed, scores, NEG_FILL)
    top = jnp.max(scores, axis=-1, keepdims=True)
    log_total = top + jnp.log(jnp.sum(jnp.exp(scores - top), axis=-1, keepdims=True))
    probs = jnp.where(allowed, jnp.exp(scores - log_total), 0.0)
    probs_low = probs.astype(BF)
    mixed = (
        jnp.einsum("mgqs,msd->mqgd", probs_low, v, preferred_element_type=F32)
        .astype(BF)
        .reshape(group_rows, q_cols)
    )
    branch_part = dot_right(mixed, wo).astype(BF).reshape(micro, 4, slots, width)
    branch = scatter_yc([branch_part[:, i] for i in range(4)]).reshape(rows, width)

    own_x = tokens.astype(F32).reshape(rows, width)
    first_scale = lax.rsqrt(jnp.mean(own_x * own_x, axis=-1, keepdims=True) + EPS_NORM)
    first_hat = own_x * first_scale
    middle = own_x + branch
    second_scale = lax.rsqrt(jnp.mean(middle * middle, axis=-1, keepdims=True) + EPS_NORM)
    second_hat = middle * second_scale
    second_normalized = (second_hat * gain_two).astype(BF)

    second_normalized, gate_up_mine, down_local = tie(
        second_normalized, gate_up_mine, by_chunk(w_down)
    )
    second_normalized, down_mine = tie(second_normalized, exchange(down_local))
    xn2_around = [second_normalized, ring(second_normalized, size)]
    for s in range(2, size):
        come = ring(xn2_around[-1], size)
        if s == 2:
            come, gate_up_over, down_mine = tie(come, gate_up_over, down_mine)
        xn2_around.append(come)
    down_over = swap(down_mine, "x")
    wgu = put_rows(put_rows(empty_rows(2 * chunk), gate_up_mine, x), gate_up_over, 1 - x)
    wd = put_rows(put_rows(empty_rows(chunk), down_mine, x), down_over, 1 - x)
    wgu = wgu.reshape(width, 2 * chunk)
    wd = wd.reshape(width, chunk)
    xn2_blocks = [b for near in xn2_around for b in (near, swap(near, "y"))]
    dfb_blocks = [b for pair in zip(dfb_around, dfb_over) for b in pair]

    halves = []
    for part in (slice(0, -2), slice(-2, None)):
        xn2 = jnp.concatenate(xn2_blocks[part], axis=0)
        dfb = jnp.concatenate(dfb_blocks[part], axis=0)
        if halves:
            xn2, *halves[0] = tie(xn2, *halves[0])
        gate_up = dot(xn2, wgu)
        gate, up = gate_up[:, :chunk], gate_up[:, chunk:]
        sigmoid = jax.nn.sigmoid(gate)
        activated = gate * sigmoid
        hidden = (activated * up).astype(BF)
        dhid = dot(dfb, wd)
        dgu = jnp.concatenate(
            [
                (dhid * up * sigmoid * (1.0 + gate * (1.0 - sigmoid))).astype(BF),
                (dhid * activated).astype(BF),
            ],
            axis=1,
        )
        if halves:
            ahead = halves[0][4].reshape(size - 1, 2, rows, width)[1]
            first_total = (ahead[0].astype(F32) + swap(ahead[1], "y")).astype(BF)
            first_total, dgu = tie(first_total, dgu)
        dxn2_part = dot_right(dgu, wgu).astype(BF)
        halves.append([xn2, dfb, hidden, dgu, dxn2_part])

    def pieces(parts):
        parts = [p.reshape(-1, 2, rows, width) for p in parts]
        return [[p[s, i] for p in parts for s in range(p.shape[0])] for i in range(2)]

    def over_cores(grad, pieces):
        grad = grad.reshape(size, 2, 2, 2, own_rows, grad.shape[1])
        sums = []
        for i in range(0, size, size // pieces):
            part = grad[i : i + size // pieces]
            sums.append((pick(part, c, 3).astype(F32) + swap(pick(part, 1 - c, 3), "c")).astype(BF))
        return jnp.concatenate(sums, axis=0)

    def over_x(grad):
        total = (pick(grad, x, 1).astype(F32) + swap(pick(grad, 1 - x, 1), "x")).astype(BF)
        return total.reshape(2 * size, own_rows, grad.shape[-1])

    (xn2_a, dfb_a, hidden_a, dgu_a, dxn2_a), (xn2_b, dfb_b, hidden_b, dgu_b, dxn2_b) = halves
    own, away = pieces([dxn2_a, dxn2_b])
    order = [(step + 1) % size for step in range(1, size)]
    away[order[0]], first_total = tie(away[order[0]], first_total)
    got = swap_in_turn([away[s] for s in order], "y")
    dxn2_b, hidden_b, dfb_a, xn2_a = tie(dxn2_b, hidden_b, dfb_a, xn2_a)
    down_grad = (dot_rows(dfb_a, hidden_a) + dot_rows(dfb_b, hidden_b)).astype(BF)
    total = first_total
    for step in range(1, size):
        total = own[order[step - 1]].astype(F32) + got[step - 1] + ring(total, size)
        if step < size - 1:
            total = total.astype(BF)
        if step == 1:
            total, down_grad, xn2_a = tie(total, down_grad, xn2_a)
            down_near = over_cores(down_grad, 2)
            gate_up_grad = dot_rows(xn2_a, dgu_a)
        if step == size - 2:
            total, gate_up_grad = tie(total, gate_up_grad)
            gate_up_grad = (gate_up_grad + dot_rows(xn2_b, dgu_b)).astype(BF)
    feed_a, feed_b = dot_right(hidden_a, wd).astype(BF), dot_right(hidden_b, wd).astype(BF)
    down_sum = over_x(down_near)
    dxn2, gate_up_grad, feed_a, feed_b = tie(total, gate_up_grad, feed_a, feed_b)
    gate_up_near = over_cores(gate_up_grad, 4)

    dh1 = dy + norm_backward(second_hat, second_scale, dxn2 * gain_two)
    dab_blocks = gather_yc(dh1.astype(BF).reshape(micro, slots, width))
    dab_blocks[2], down_sum, gate_up_near = tie(dab_blocks[2], down_sum, gate_up_near)
    gate_up_sum = over_x(gate_up_near)
    down_parts = exchange(down_sum)
    dab_blocks[3], feed_a, feed_b = tie(dab_blocks[3], feed_a, feed_b)
    dab = jnp.concatenate(dab_blocks, axis=1).reshape(group_rows, width)

    def blocks_of(*grads):
        grads = [g.reshape(size, 2, block_rows, g.shape[1]) for g in grads]
        at = [[pick(g, behind(s)) for g in grads] for s in range(size)]
        return [
            [jnp.concatenate([pick(g, i) for g in gs], axis=1) for gs in at] for i in (x, 1 - x)
        ]

    out_grad_part = dot_rows(dab, mixed).astype(BF)

    dob = dot(dab, wo).astype(BF)
    dob = dob.reshape(micro, span, q_heads, HEAD_DIMENSION)
    dprob = jnp.einsum("mqgd,msd->mgqs", dob, v, preferred_element_type=F32)
    dscore = (probs * (dprob - jnp.sum(probs * dprob, axis=-1, keepdims=True))).astype(BF)
    dq = jnp.einsum("mgqs,msd->mqgd", dscore, k, preferred_element_type=F32) * scale
    dk = jnp.einsum("mgqs,mqgd->msd", dscore, q, preferred_element_type=F32) * scale
    dv = jnp.einsum("mgqs,mqgd->msd", probs_low, dob, preferred_element_type=F32)
    dq = rotary_backward(dq, cosine, sine).astype(BF).reshape(group_rows, q_cols)
    dk = rotary_backward(dk[:, :, None, :], cosine, sine).astype(BF).reshape(group_rows, kv_cols)
    dqkv = jnp.concatenate([dq, dk, dv.astype(BF).reshape(group_rows, kv_cols)], axis=1)

    feed = scatter_z(*pieces([feed_a, feed_b]), "y", size)
    outputs = (live * (middle + feed)).astype(BF)
    head_own, head_away = blocks_of(dot_rows(xn1, dqkv).astype(BF), out_grad_part)
    order = [(step + 1) % size for step in range(size)]
    head_away[order[0]], gate_up_sum = tie(head_away[order[0]], gate_up_sum)
    head_got = swap_in_turn([head_away[s] for s in order], "x")
    gate_parts = exchange(gate_up_sum[:, :, :chunk])
    head_got[-1], up_sum = tie(head_got[-1], gate_up_sum[:, :, chunk:])
    up_parts = exchange(up_sum)
    head_sum = head_own[order[0]].astype(F32) + head_got[0]
    for step in range(1, size):
        head_sum = head_sum.astype(BF)
        if step == size - 1:
            head_sum, outputs = tie(head_sum, outputs)
        head_sum = head_own[order[step]].astype(F32) + head_got[step] + ring(head_sum, size)
    outputs = outputs.reshape(hidden_in.shape)

    dxn1_part = dot_right(dqkv, wqkv).astype(BF).reshape(micro, 4, slots, width)
    dxn1 = scatter_yc([dxn1_part[:, i] for i in range(4)]).reshape(rows, width)
    input_grads = (
        (dh1 + norm_backward(first_hat, first_scale, dxn1 * gain_one))
        .astype(BF)
        .reshape(hidden_in.shape)
    )

    def owned(block):
        block = block.astype(BF)
        came = to_peers_yc(lambda k: cut(block, (j ^ k) * own_rows, own_rows, 0))
        heads = jnp.zeros((4, own_rows, block.shape[1]), BF)
        for k in range(4):
            heads = put(heads, came[k], j ^ k)
        return heads

    def side_by_side(parts, start, count):
        return jnp.concatenate(
            [parts[i, :, start : start + count] for i in range(parts.shape[0])], axis=1
        ).astype(F32)

    heads = owned(head_sum)
    grad_query = side_by_side(heads, 0, q_cols)
    grad_key = side_by_side(heads, q_cols, kv_cols)
    grad_value = side_by_side(heads, q_cols + kv_cols, kv_cols)
    grad_out = side_by_side(heads, qkv_cols, q_cols)
    grad_gate = side_by_side(gate_parts, 0, chunk)
    grad_up = side_by_side(up_parts, 0, chunk)
    grad_down = side_by_side(down_parts, 0, chunk)

    def gain_gradient(gain, *pairs):
        total = sum(jnp.sum(w.astype(F32) * g, axis=1) for w, g in pairs)
        return total / gain.astype(F32)

    grad_attn_gain = gain_gradient(
        attn_gain, (w_query, grad_query), (key_matrix, grad_key), (value_matrix, grad_value)
    )
    grad_mlp_gain = gain_gradient(mlp_gain, (w_gate, grad_gate), (w_up, grad_up))
    return (
        outputs,
        input_grads,
        grad_attn_gain,
        grad_query,
        grad_key,
        grad_value,
        grad_out,
        grad_mlp_gain,
        grad_gate,
        grad_up,
        grad_down,
    )


def solution(mesh):
    dp, fsdp = mesh.shape["dp"], mesh.shape["fsdp"]
    fine = Mesh(mesh.devices.reshape(dp // 2, 2, fsdp // 2, 2), ("z", "x", "y", "c"))
    batch, slot, both = ("z", "x"), ("y", "c"), ("z", "x", "y", "c")
    vector, matrix = P(both), P(both, None)
    rows = P(None, batch, slot, None)
    return jax.shard_map(
        per_device,
        mesh=fine,
        in_specs=(rows, P(None, batch), rows) + (vector,) + (matrix,) * 4 + (vector,) + (matrix,) * 3,
        out_specs=(rows, rows, vector) + (matrix,) * 4 + (vector,) + (matrix,) * 3,
        check_vma=False,
    )
```

```python
import jax
import jax.numpy as jnp
from jax import lax
from jax.sharding import Mesh, PartitionSpec as P

QUERY_HEADS = 8
KEY_VALUE_HEADS = 4
HEAD_DIMENSION = 256

EPS_NORM = 1e-06
ROPE_BASE = 1000042.0
NEG_FILL = -1e30

BF = jnp.bfloat16
F32 = jnp.float32


def rope_tables(positions, head_size):
    half_size = head_size // 2
    inverse = ROPE_BASE ** (-(jnp.arange(half_size, dtype=F32) * 2.0 / head_size))
    angles = positions.astype(F32)[:, None] * inverse[None, :]
    return jnp.cos(angles), jnp.sin(angles)


def rotary_embed(rows, cosine, sine):
    half = rows.shape[-1] // 2
    first, second = rows[..., :half], rows[..., half:]
    return jnp.concatenate(
        [first * cosine - second * sine, second * cosine + first * sine], axis=-1
    )


def rotary_backward(grads, cosine, sine):
    half = grads.shape[-1] // 2
    first, second = grads[..., :half], grads[..., half:]
    return jnp.concatenate(
        [first * cosine + second * sine, second * cosine - first * sine], axis=-1
    )


def norm_backward(normalized, reciprocal, gradient):
    return reciprocal * (
        gradient - normalized * jnp.mean(gradient * normalized, axis=-1, keepdims=True)
    )


def dot(left, right):
    return jnp.dot(left, right, preferred_element_type=F32)


def dot_right(left, right):
    return lax.dot_general(left, right, (((1,), (1,)), ((), ())), preferred_element_type=F32)


def dot_rows(left, right):
    return lax.dot_general(left, right, (((0,), (0,)), ((), ())), preferred_element_type=F32)


def swap(value, axis):
    return lax.ppermute(value, axis, [(0, 1), (1, 0)])


def ring(value, size):
    return lax.ppermute(value, "z", [(i, (i + 1) % size) for i in range(size)])


def pick(value, index, axis=0):
    return lax.dynamic_index_in_dim(value, index, axis, keepdims=False)


def put(buffer, piece, *index):
    piece = piece.reshape((1,) * len(index) + piece.shape)
    starts = tuple(index) + (0,) * (buffer.ndim - len(index))
    return lax.dynamic_update_slice(buffer, piece, starts)


def tie(*values):
    return lax.optimization_barrier(values)


def cut(value, start, count, axis):
    return lax.dynamic_slice_in_dim(value, start, count, axis)


def swap_cores(blocks):
    return [[swap(b[i], "c") for i in range(b.shape[0])] for b in blocks]


def gather_yc(block, across=None):
    if across is None:
        across = swap(block, "y")
    near, far = (jnp.stack(b) for b in swap_cores([block, across]))
    return [block, near, across, far]


def scatter_yc(parts):
    far, near = (jnp.stack(b) for b in swap_cores([parts[3], parts[1]]))
    away = (parts[2].astype(F32) + far).astype(BF)
    return parts[0].astype(F32) + near + swap(away, "y")


def to_peers_yc(piece_for):
    pieces = [piece_for(0)]
    for k in range(1, 4):
        pieces.append(lax.ppermute(piece_for(k), ("y", "c"), [(i, i ^ k) for i in range(4)]))
    return pieces


def swap_in_turn(pieces, axis):
    got = []
    for piece in pieces:
        if got:
            piece, got[-1] = tie(piece, got[-1])
        got.append(swap(piece, axis))
    return got


def scatter_z(parts, partners, axis, size, ties=None):
    total = None
    order = [(step + 1) % size for step in range(size)]
    got = swap_in_turn([partners[s] for s in order], axis)
    for step in range(size):
        own = parts[order[step]].astype(F32) + got[step]
        total = own if total is None else own + ring(total, size)
        if step < size - 1:
            total = total.astype(BF)
            if ties and step in ties:
                total, *ties[step] = tie(total, *ties[step])
    return total


def per_device(
    hidden_in,
    seq_lengths,
    out_grad,
    attn_gain,
    w_query,
    key_matrix,
    value_matrix,
    w_out,
    mlp_gain,
    w_gate,
    w_up,
    w_down,
):
    micro, _, slots, width = hidden_in.shape
    size = lax.axis_size("z")
    z, x, y, c = (lax.axis_index(a) for a in ("z", "x", "y", "c"))
    j = y * 2 + c
    own_rows = w_query.shape[0]
    block_rows = 4 * own_rows
    q_cols = w_query.shape[1] // 4
    kv_cols = key_matrix.shape[1] // 4
    qkv_cols = q_cols + 2 * kv_cols
    ff = w_gate.shape[1]
    chunk = ff // (2 * size)
    rows = micro * slots
    group_rows = 4 * rows
    span = 4 * slots
    q_heads = q_cols // HEAD_DIMENSION
    scale = HEAD_DIMENSION ** (-0.5)
    lengths = seq_lengths.reshape(micro)

    def behind(s):
        return lax.rem(z - s + size, size)

    def by_chunk(weight):
        return jnp.swapaxes(weight.reshape(own_rows, 2 * size, chunk), 0, 1)

    def exchange(parts):
        return lax.all_to_all(parts, ("z", "y"), 0, 0, tiled=True)

    offsets = jnp.arange(slots, dtype=jnp.int32)
    own_slots = j * slots + offsets
    live = (own_slots[None, :] < lengths[:, None]).astype(F32).reshape(rows, 1)
    dy = out_grad.astype(F32).reshape(rows, width) * live
    dfb_around = [dy.astype(BF)]
    dfb_around.append(ring(dfb_around[-1], size))

    def beside(values, columns):
        return jnp.pad(values, ((0, 8 - values.shape[0]), (0, columns - values.shape[1])))

    gains = jnp.stack([attn_gain, mlp_gain])

    def head_piece(k):
        to = j ^ k
        weights = jnp.concatenate(
            [
                cut(w_query, to * q_cols, q_cols, 1),
                cut(key_matrix, to * kv_cols, kv_cols, 1),
                cut(value_matrix, to * kv_cols, kv_cols, 1),
                cut(w_out, to * q_cols, q_cols, 1),
            ],
            axis=1,
        )
        return jnp.concatenate([weights, beside(gains, weights.shape[1])], axis=0)

    head_pieces = to_peers_yc(head_piece)

    head_cols = qkv_cols + q_cols
    block = jnp.zeros((4, own_rows, head_cols), BF)
    gain_block = jnp.zeros((4, 2, own_rows), BF)
    for k, piece in enumerate(head_pieces):
        block = put(block, piece[:own_rows], j ^ k)
        gain_block = put(gain_block, piece[own_rows : own_rows + 2, :own_rows], j ^ k)
    gain_block = jnp.swapaxes(gain_block, 0, 1).reshape(2, block_rows)
    block = jnp.concatenate(
        [block.reshape(block_rows, head_cols), beside(gain_block, head_cols)], axis=0
    )

    block, dfb_around[1], dfb_here, hidden_in, w_gate, w_up, w_down = tie(
        block, dfb_around[1], dfb_around[0], hidden_in, w_gate, w_up, w_down
    )
    tokens = hidden_in.reshape(micro, slots, width)
    around, over = [block], []
    across = swap(tokens, "y")
    dfb_here, across = tie(dfb_here, across)
    token_blocks = gather_yc(tokens, across)
    for s in range(1, size):
        over.append(swap(around[-1], "x"))
        around.append(ring(around[-1], size))
        around[s], over[s - 1] = tie(around[s], over[s - 1])
        if s > 1:
            dfb_around.append(ring(dfb_around[-1], size))
        if s == size - 2:
            around[s], *token_blocks = tie(around[s], *token_blocks)
    dfb_over = swap_in_turn([dfb_here, *dfb_around[1:]], "y")
    gate_up_local = jnp.concatenate([by_chunk(w_gate), by_chunk(w_up)], axis=2)
    gate_up_local, around[-1], *dfb_over[:-1] = tie(gate_up_local, around[-1], *dfb_over[:-1])
    gate_up_mine = exchange(gate_up_local)
    over.append(swap(around[-1], "x"))
    gate_up_over = swap(gate_up_mine, "x")

    wqkv = jnp.zeros((size, 2, block_rows, qkv_cols), BF)
    gains_all = jnp.zeros((size, 2, 2, block_rows), BF)
    wo = jnp.zeros((size, 2, block_rows, q_cols), BF)
    for s in range(size):
        for at, piece in ((x, around[s]), (1 - x, over[s])):
            wqkv = put(wqkv, piece[:block_rows, :qkv_cols], behind(s), at)
            wo = put(wo, piece[:block_rows, qkv_cols:], behind(s), at)
            gains_all = put(gains_all, piece[block_rows : block_rows + 2, :block_rows], behind(s), at)
    wqkv = wqkv.reshape(width, qkv_cols)
    wo = wo.reshape(width, q_cols)
    gain_one = gains_all[:, :, 0].astype(F32).reshape(1, width)
    gain_two = gains_all[:, :, 1].astype(F32).reshape(1, width)

    def put_rows(whole, piece, at):
        piece = piece.reshape(size, 1, 2, 1, own_rows, piece.shape[2])
        whole = lax.dynamic_update_slice(whole, piece, (0, at, 0, c, 0, 0))
        for i in range(0, size, size // 4):
            part = swap(piece[i : i + size // 4], "c")
            whole = lax.dynamic_update_slice(whole, part, (i, at, 0, 1 - c, 0, 0))
        return whole

    def empty_rows(columns):
        return jnp.zeros((size, 2, 2, 2, own_rows, columns), BF)

    positions = jnp.concatenate([(j ^ k) * slots + offsets for k in range(4)])
    cosine, sine = rope_tables(positions, HEAD_DIMENSION)
    cosine, sine = cosine[None, :, None, :], sine[None, :, None, :]
    all_x = jnp.concatenate(token_blocks, axis=1).astype(F32).reshape(group_rows, width)
    all_scale = lax.rsqrt(jnp.mean(all_x * all_x, axis=-1, keepdims=True) + EPS_NORM)
    xn1 = (all_x * all_scale * gain_one).astype(BF)
    qkv = dot(xn1, wqkv)
    q = rotary_embed(
        qkv[:, :q_cols].reshape(micro, span, q_heads, HEAD_DIMENSION), cosine, sine
    ).astype(BF)
    k = rotary_embed(
        qkv[:, q_cols : q_cols + kv_cols].reshape(micro, span, 1, HEAD_DIMENSION), cosine, sine
    ).astype(BF)[:, :, 0]
    v = qkv[:, q_cols + kv_cols :].reshape(micro, span, HEAD_DIMENSION).astype(BF)
    allowed = (positions[None, None, :] <= positions[None, :, None]) & (
        positions[None, None, :] < lengths[:, None, None]
    )
    allowed = allowed[:, None, :, :]
    scores = jnp.einsum("mqgd,msd->mgqs", q, k, preferred_element_type=F32) * scale
    scores = jnp.where(allowed, scores, NEG_FILL)
    top = jnp.max(scores, axis=-1, keepdims=True)
    log_total = top + jnp.log(jnp.sum(jnp.exp(scores - top), axis=-1, keepdims=True))
    probs = jnp.where(allowed, jnp.exp(scores - log_total), 0.0)
    probs_low = probs.astype(BF)
    mixed = (
        jnp.einsum("mgqs,msd->mqgd", probs_low, v, preferred_element_type=F32)
        .astype(BF)
        .reshape(group_rows, q_cols)
    )
    branch_part = dot_right(mixed, wo).astype(BF).reshape(micro, 4, slots, width)
    branch = scatter_yc([branch_part[:, i] for i in range(4)]).reshape(rows, width)

    own_x = tokens.astype(F32).reshape(rows, width)
    first_scale = lax.rsqrt(jnp.mean(own_x * own_x, axis=-1, keepdims=True) + EPS_NORM)
    first_hat = own_x * first_scale
    middle = own_x + branch
    second_scale = lax.rsqrt(jnp.mean(middle * middle, axis=-1, keepdims=True) + EPS_NORM)
    second_hat = middle * second_scale
    second_normalized = (second_hat * gain_two).astype(BF)

    second_normalized, gate_up_mine, down_local = tie(
        second_normalized, gate_up_mine, by_chunk(w_down)
    )
    second_normalized, down_mine = tie(second_normalized, exchange(down_local))
    xn2_around = [second_normalized, ring(second_normalized, size)]
    for s in range(2, size):
        come = ring(xn2_around[-1], size)
        if s == 2:
            come, gate_up_over, down_mine = tie(come, gate_up_over, down_mine)
        xn2_around.append(come)
    down_over = swap(down_mine, "x")
    wgu = put_rows(put_rows(empty_rows(2 * chunk), gate_up_mine, x), gate_up_over, 1 - x)
    wd = put_rows(put_rows(empty_rows(chunk), down_mine, x), down_over, 1 - x)
    wgu = wgu.reshape(width, 2 * chunk)
    wd = wd.reshape(width, chunk)
    xn2_blocks = [b for near in xn2_around for b in (near, swap(near, "y"))]
    dfb_blocks = [b for pair in zip(dfb_around, dfb_over) for b in pair]

    halves = []
    for part in (slice(0, -2), slice(-2, None)):
        xn2 = jnp.concatenate(xn2_blocks[part], axis=0)
        dfb = jnp.concatenate(dfb_blocks[part], axis=0)
        if halves:
            xn2, *halves[0] = tie(xn2, *halves[0])
        gate_up = dot(xn2, wgu)
        gate, up = gate_up[:, :chunk], gate_up[:, chunk:]
        sigmoid = jax.nn.sigmoid(gate)
        activated = gate * sigmoid
        hidden = (activated * up).astype(BF)
        dhid = dot(dfb, wd)
        dgu = jnp.concatenate(
            [
                (dhid * up * sigmoid * (1.0 + gate * (1.0 - sigmoid))).astype(BF),
                (dhid * activated).astype(BF),
            ],
            axis=1,
        )
        if halves:
            ahead = halves[0][4].reshape(size - 1, 2, rows, width)[1]
            first_total = (ahead[0].astype(F32) + swap(ahead[1], "y")).astype(BF)
            first_total, dgu = tie(first_total, dgu)
        dxn2_part = dot_right(dgu, wgu).astype(BF)
        halves.append([xn2, dfb, hidden, dgu, dxn2_part])

    def pieces(parts):
        parts = [p.reshape(-1, 2, rows, width) for p in parts]
        return [[p[s, i] for p in parts for s in range(p.shape[0])] for i in range(2)]

    def over_cores(grad, pieces):
        grad = grad.reshape(size, 2, 2, 2, own_rows, grad.shape[1])
        sums = []
        for i in range(0, size, size // pieces):
            part = grad[i : i + size // pieces]
            sums.append((pick(part, c, 3).astype(F32) + swap(pick(part, 1 - c, 3), "c")).astype(BF))
        return jnp.concatenate(sums, axis=0)

    def over_x(grad):
        total = (pick(grad, x, 1).astype(F32) + swap(pick(grad, 1 - x, 1), "x")).astype(BF)
        return total.reshape(2 * size, own_rows, grad.shape[-1])

    (xn2_a, dfb_a, hidden_a, dgu_a, dxn2_a), (xn2_b, dfb_b, hidden_b, dgu_b, dxn2_b) = halves
    own, away = pieces([dxn2_a, dxn2_b])
    order = [(step + 1) % size for step in range(1, size)]
    away[order[0]], first_total = tie(away[order[0]], first_total)
    got = swap_in_turn([away[s] for s in order], "y")
    dxn2_b, hidden_b, dfb_a, xn2_a = tie(dxn2_b, hidden_b, dfb_a, xn2_a)
    down_grad = (dot_rows(dfb_a, hidden_a) + dot_rows(dfb_b, hidden_b)).astype(BF)
    total = first_total
    for step in range(1, size):
        total = own[order[step - 1]].astype(F32) + got[step - 1] + ring(total, size)
        if step < size - 1:
            total = total.astype(BF)
        if step == 1:
            total, down_grad, xn2_a = tie(total, down_grad, xn2_a)
            down_near = over_cores(down_grad, 2)
            gate_up_grad = dot_rows(xn2_a, dgu_a)
        if step == size - 2:
            total, gate_up_grad = tie(total, gate_up_grad)
            gate_up_grad = (gate_up_grad + dot_rows(xn2_b, dgu_b)).astype(BF)
    feed_a, feed_b = dot_right(hidden_a, wd).astype(BF), dot_right(hidden_b, wd).astype(BF)
    down_sum = over_x(down_near)
    dxn2, gate_up_grad, feed_a, feed_b = tie(total, gate_up_grad, feed_a, feed_b)
    gate_up_near = over_cores(gate_up_grad, 4)

    dh1 = dy + norm_backward(second_hat, second_scale, dxn2 * gain_two)
    dab_blocks = gather_yc(dh1.astype(BF).reshape(micro, slots, width))
    dab_blocks[2], down_sum, gate_up_near = tie(dab_blocks[2], down_sum, gate_up_near)
    gate_up_sum = over_x(gate_up_near)
    down_parts = exchange(down_sum)
    dab_blocks[3], feed_a, feed_b = tie(dab_blocks[3], feed_a, feed_b)
    dab = jnp.concatenate(dab_blocks, axis=1).reshape(group_rows, width)

    def blocks_of(*grads):
        grads = [g.reshape(size, 2, block_rows, g.shape[1]) for g in grads]
        at = [[pick(g, behind(s)) for g in grads] for s in range(size)]
        return [
            [jnp.concatenate([pick(g, i) for g in gs], axis=1) for gs in at] for i in (x, 1 - x)
        ]

    out_grad_part = dot_rows(dab, mixed).astype(BF)

    dob = dot(dab, wo).astype(BF)
    dob = dob.reshape(micro, span, q_heads, HEAD_DIMENSION)
    dprob = jnp.einsum("mqgd,msd->mgqs", dob, v, preferred_element_type=F32)
    dscore = (probs * (dprob - jnp.sum(probs * dprob, axis=-1, keepdims=True))).astype(BF)
    dq = jnp.einsum("mgqs,msd->mqgd", dscore, k, preferred_element_type=F32) * scale
    dk = jnp.einsum("mgqs,mqgd->msd", dscore, q, preferred_element_type=F32) * scale
    dv = jnp.einsum("mgqs,mqgd->msd", probs_low, dob, preferred_element_type=F32)
    dq = rotary_backward(dq, cosine, sine).astype(BF).reshape(group_rows, q_cols)
    dk = rotary_backward(dk[:, :, None, :], cosine, sine).astype(BF).reshape(group_rows, kv_cols)
    dqkv = jnp.concatenate([dq, dk, dv.astype(BF).reshape(group_rows, kv_cols)], axis=1)

    feed = scatter_z(*pieces([feed_a, feed_b]), "y", size)
    outputs = (live * (middle + feed)).astype(BF)
    head_own, head_away = blocks_of(dot_rows(xn1, dqkv).astype(BF), out_grad_part)
    order = [(step + 1) % size for step in range(size)]
    head_away[order[0]], gate_up_sum = tie(head_away[order[0]], gate_up_sum)
    head_got = swap_in_turn([head_away[s] for s in order], "x")
    gate_parts = exchange(gate_up_sum[:, :, :chunk])
    head_got[-1], up_sum = tie(head_got[-1], gate_up_sum[:, :, chunk:])
    up_parts = exchange(up_sum)
    head_sum = head_own[order[0]].astype(F32) + head_got[0]
    for step in range(1, size):
        head_sum = head_sum.astype(BF)
        if step == size - 1:
            head_sum, outputs = tie(head_sum, outputs)
        head_sum = head_own[order[step]].astype(F32) + head_got[step] + ring(head_sum, size)
    outputs = outputs.reshape(hidden_in.shape)

    dxn1_part = dot_right(dqkv, wqkv).astype(BF).reshape(micro, 4, slots, width)
    dxn1 = scatter_yc([dxn1_part[:, i] for i in range(4)]).reshape(rows, width)
    input_grads = (
        (dh1 + norm_backward(first_hat, first_scale, dxn1 * gain_one))
        .astype(BF)
        .reshape(hidden_in.shape)
    )

    def owned(block):
        block = block.astype(BF)
        came = to_peers_yc(lambda k: cut(block, (j ^ k) * own_rows, own_rows, 0))
        heads = jnp.zeros((4, own_rows, block.shape[1]), BF)
        for k in range(4):
            heads = put(heads, came[k], j ^ k)
        return heads

    def side_by_side(parts, start, count):
        return jnp.concatenate(
            [parts[i, :, start : start + count] for i in range(parts.shape[0])], axis=1
        ).astype(F32)

    heads = owned(head_sum)
    grad_query = side_by_side(heads, 0, q_cols)
    grad_key = side_by_side(heads, q_cols, kv_cols)
    grad_value = side_by_side(heads, q_cols + kv_cols, kv_cols)
    grad_out = side_by_side(heads, qkv_cols, q_cols)
    grad_gate = side_by_side(gate_parts, 0, chunk)
    grad_up = side_by_side(up_parts, 0, chunk)
    grad_down = side_by_side(down_parts, 0, chunk)

    def gain_gradient(gain, *pairs):
        total = sum(jnp.sum(w.astype(F32) * g, axis=1) for w, g in pairs)
        return total / gain.astype(F32)

    grad_attn_gain = gain_gradient(
        attn_gain, (w_query, grad_query), (key_matrix, grad_key), (value_matrix, grad_value)
    )
    grad_mlp_gain = gain_gradient(mlp_gain, (w_gate, grad_gate), (w_up, grad_up))
    return (
        outputs,
        input_grads,
        grad_attn_gain,
        grad_query,
        grad_key,
        grad_value,
        grad_out,
        grad_mlp_gain,
        grad_gate,
        grad_up,
        grad_down,
    )


def solution(mesh):
    dp, fsdp = mesh.shape["dp"], mesh.shape["fsdp"]
    fine = Mesh(mesh.devices.reshape(dp // 2, 2, fsdp // 2, 2), ("z", "x", "y", "c"))
    batch, slot, both = ("z", "x"), ("y", "c"), ("z", "x", "y", "c")
    vector, matrix = P(both), P(both, None)
    rows = P(None, batch, slot, None)
    return jax.shard_map(
        per_device,
        mesh=fine,
        in_specs=(rows, P(None, batch), rows) + (vector,) + (matrix,) * 4 + (vector,) + (matrix,) * 3,
        out_specs=(rows, rows, vector) + (matrix,) * 4 + (vector,) + (matrix,) * 3,
        check_vma=False,
    )
```

```python
import jax
import jax.numpy as jnp
from jax import lax
from jax.sharding import Mesh, PartitionSpec as P

QUERY_HEADS = 8
KEY_VALUE_HEADS = 4
HEAD_DIMENSION = 256

EPS_NORM = 1e-06
ROPE_BASE = 1000042.0
NEG_FILL = -1e30

BF = jnp.bfloat16
F32 = jnp.float32


def rope_tables(positions, head_size):
    half_size = head_size // 2
    inverse = ROPE_BASE ** (-(jnp.arange(half_size, dtype=F32) * 2.0 / head_size))
    angles = positions.astype(F32)[:, None] * inverse[None, :]
    return jnp.cos(angles), jnp.sin(angles)


def rotary_embed(rows, cosine, sine):
    half = rows.shape[-1] // 2
    first, second = rows[..., :half], rows[..., half:]
    return jnp.concatenate(
        [first * cosine - second * sine, second * cosine + first * sine], axis=-1
    )


def rotary_backward(grads, cosine, sine):
    half = grads.shape[-1] // 2
    first, second = grads[..., :half], grads[..., half:]
    return jnp.concatenate(
        [first * cosine + second * sine, second * cosine - first * sine], axis=-1
    )


def norm_backward(normalized, reciprocal, gradient):
    return reciprocal * (
        gradient - normalized * jnp.mean(gradient * normalized, axis=-1, keepdims=True)
    )


def dot(left, right):
    return jnp.dot(left, right, preferred_element_type=F32)


def dot_right(left, right):
    return lax.dot_general(left, right, (((1,), (1,)), ((), ())), preferred_element_type=F32)


def dot_rows(left, right):
    return lax.dot_general(left, right, (((0,), (0,)), ((), ())), preferred_element_type=F32)


def swap(value, axis):
    return lax.ppermute(value, axis, [(0, 1), (1, 0)])


def ring(value, size):
    return lax.ppermute(value, "z", [(i, (i + 1) % size) for i in range(size)])


def pick(value, index, axis=0):
    return lax.dynamic_index_in_dim(value, index, axis, keepdims=False)


def put(buffer, piece, *index):
    piece = piece.reshape((1,) * len(index) + piece.shape)
    starts = tuple(index) + (0,) * (buffer.ndim - len(index))
    return lax.dynamic_update_slice(buffer, piece, starts)


def tie(*values):
    return lax.optimization_barrier(values)


def cut(value, start, count, axis):
    return lax.dynamic_slice_in_dim(value, start, count, axis)


def swap_cores(blocks):
    return [[swap(b[i], "c") for i in range(b.shape[0])] for b in blocks]


def gather_yc(block, across=None):
    if across is None:
        across = swap(block, "y")
    near, far = (jnp.stack(b) for b in swap_cores([block, across]))
    return [block, near, across, far]


def scatter_yc(parts):
    far, near = (jnp.stack(b) for b in swap_cores([parts[3], parts[1]]))
    away = (parts[2].astype(F32) + far).astype(BF)
    return parts[0].astype(F32) + near + swap(away, "y")


def to_peers_yc(piece_for):
    pieces = [piece_for(0)]
    for k in range(1, 4):
        pieces.append(lax.ppermute(piece_for(k), ("y", "c"), [(i, i ^ k) for i in range(4)]))
    return pieces


def swap_in_turn(pieces, axis):
    got = []
    for piece in pieces:
        if got:
            piece, got[-1] = tie(piece, got[-1])
        got.append(swap(piece, axis))
    return got


def scatter_z(parts, partners, axis, size, ties=None):
    total = None
    order = [(step + 1) % size for step in range(size)]
    got = swap_in_turn([partners[s] for s in order], axis)
    for step in range(size):
        own = parts[order[step]].astype(F32) + got[step]
        total = own if total is None else own + ring(total, size)
        if step < size - 1:
            total = total.astype(BF)
            if ties and step in ties:
                total, *ties[step] = tie(total, *ties[step])
    return total


def per_device(
    hidden_in,
    seq_lengths,
    out_grad,
    attn_gain,
    w_query,
    key_matrix,
    value_matrix,
    w_out,
    mlp_gain,
    w_gate,
    w_up,
    w_down,
):
    micro, _, slots, width = hidden_in.shape
    size = lax.axis_size("z")
    z, x, y, c = (lax.axis_index(a) for a in ("z", "x", "y", "c"))
    j = y * 2 + c
    own_rows = w_query.shape[0]
    block_rows = 4 * own_rows
    q_cols = w_query.shape[1] // 4
    kv_cols = key_matrix.shape[1] // 4
    qkv_cols = q_cols + 2 * kv_cols
    ff = w_gate.shape[1]
    chunk = ff // (2 * size)
    rows = micro * slots
    group_rows = 4 * rows
    span = 4 * slots
    q_heads = q_cols // HEAD_DIMENSION
    scale = HEAD_DIMENSION ** (-0.5)
    lengths = seq_lengths.reshape(micro)

    def behind(s):
        return lax.rem(z - s + size, size)

    def by_chunk(weight):
        return jnp.swapaxes(weight.reshape(own_rows, 2 * size, chunk), 0, 1)

    def exchange(parts):
        return lax.all_to_all(parts, ("z", "y"), 0, 0, tiled=True)

    offsets = jnp.arange(slots, dtype=jnp.int32)
    own_slots = j * slots + offsets
    live = (own_slots[None, :] < lengths[:, None]).astype(F32).reshape(rows, 1)
    dy = out_grad.astype(F32).reshape(rows, width) * live
    dfb_around = [dy.astype(BF)]
    dfb_around.append(ring(dfb_around[-1], size))

    def beside(values, columns):
        return jnp.pad(values, ((0, 8 - values.shape[0]), (0, columns - values.shape[1])))

    gains = jnp.stack([attn_gain, mlp_gain])

    def head_piece(k):
        to = j ^ k
        weights = jnp.concatenate(
            [
                cut(w_query, to * q_cols, q_cols, 1),
                cut(key_matrix, to * kv_cols, kv_cols, 1),
                cut(value_matrix, to * kv_cols, kv_cols, 1),
                cut(w_out, to * q_cols, q_cols, 1),
            ],
            axis=1,
        )
        return jnp.concatenate([weights, beside(gains, weights.shape[1])], axis=0)

    head_pieces = to_peers_yc(head_piece)

    head_cols = qkv_cols + q_cols
    block = jnp.zeros((4, own_rows, head_cols), BF)
    gain_block = jnp.zeros((4, 2, own_rows), BF)
    for k, piece in enumerate(head_pieces):
        block = put(block, piece[:own_rows], j ^ k)
        gain_block = put(gain_block, piece[own_rows : own_rows + 2, :own_rows], j ^ k)
    gain_block = jnp.swapaxes(gain_block, 0, 1).reshape(2, block_rows)
    block = jnp.concatenate(
        [block.reshape(block_rows, head_cols), beside(gain_block, head_cols)], axis=0
    )

    block, dfb_around[1], dfb_here, hidden_in, w_gate, w_up, w_down = tie(
        block, dfb_around[1], dfb_around[0], hidden_in, w_gate, w_up, w_down
    )
    tokens = hidden_in.reshape(micro, slots, width)
    around, over = [block], []
    across = swap(tokens, "y")
    dfb_here, across = tie(dfb_here, across)
    token_blocks = gather_yc(tokens, across)
    for s in range(1, size):
        over.append(swap(around[-1], "x"))
        around.append(ring(around[-1], size))
        around[s], over[s - 1] = tie(around[s], over[s - 1])
        if s > 1:
            dfb_around.append(ring(dfb_around[-1], size))
        if s == size - 2:
            around[s], *token_blocks = tie(around[s], *token_blocks)
    dfb_over = swap_in_turn([dfb_here, *dfb_around[1:]], "y")
    gate_up_local = jnp.concatenate([by_chunk(w_gate), by_chunk(w_up)], axis=2)
    gate_up_local, around[-1], *dfb_over[:-1] = tie(gate_up_local, around[-1], *dfb_over[:-1])
    gate_up_mine = exchange(gate_up_local)
    over.append(swap(around[-1], "x"))
    gate_up_over = swap(gate_up_mine, "x")

    wqkv = jnp.zeros((size, 2, block_rows, qkv_cols), BF)
    gains_all = jnp.zeros((size, 2, 2, block_rows), BF)
    wo = jnp.zeros((size, 2, block_rows, q_cols), BF)
    for s in range(size):
        for at, piece in ((x, around[s]), (1 - x, over[s])):
            wqkv = put(wqkv, piece[:block_rows, :qkv_cols], behind(s), at)
            wo = put(wo, piece[:block_rows, qkv_cols:], behind(s), at)
            gains_all = put(gains_all, piece[block_rows : block_rows + 2, :block_rows], behind(s), at)
    wqkv = wqkv.reshape(width, qkv_cols)
    wo = wo.reshape(width, q_cols)
    gain_one = gains_all[:, :, 0].astype(F32).reshape(1, width)
    gain_two = gains_all[:, :, 1].astype(F32).reshape(1, width)

    def put_rows(whole, piece, at):
        piece = piece.reshape(size, 1, 2, 1, own_rows, piece.shape[2])
        whole = lax.dynamic_update_slice(whole, piece, (0, at, 0, c, 0, 0))
        for i in range(0, size, size // 4):
            part = swap(piece[i : i + size // 4], "c")
            whole = lax.dynamic_update_slice(whole, part, (i, at, 0, 1 - c, 0, 0))
        return whole

    def empty_rows(columns):
        return jnp.zeros((size, 2, 2, 2, own_rows, columns), BF)

    positions = jnp.concatenate([(j ^ k) * slots + offsets for k in range(4)])
    cosine, sine = rope_tables(positions, HEAD_DIMENSION)
    cosine, sine = cosine[None, :, None, :], sine[None, :, None, :]
    all_x = jnp.concatenate(token_blocks, axis=1).astype(F32).reshape(group_rows, width)
    all_scale = lax.rsqrt(jnp.mean(all_x * all_x, axis=-1, keepdims=True) + EPS_NORM)
    xn1 = (all_x * all_scale * gain_one).astype(BF)
    qkv = dot(xn1, wqkv)
    q = rotary_embed(
        qkv[:, :q_cols].reshape(micro, span, q_heads, HEAD_DIMENSION), cosine, sine
    ).astype(BF)
    k = rotary_embed(
        qkv[:, q_cols : q_cols + kv_cols].reshape(micro, span, 1, HEAD_DIMENSION), cosine, sine
    ).astype(BF)[:, :, 0]
    v = qkv[:, q_cols + kv_cols :].reshape(micro, span, HEAD_DIMENSION).astype(BF)
    allowed = (positions[None, None, :] <= positions[None, :, None]) & (
        positions[None, None, :] < lengths[:, None, None]
    )
    allowed = allowed[:, None, :, :]
    scores = jnp.einsum("mqgd,msd->mgqs", q, k, preferred_element_type=F32) * scale
    scores = jnp.where(allowed, scores, NEG_FILL)
    top = jnp.max(scores, axis=-1, keepdims=True)
    log_total = top + jnp.log(jnp.sum(jnp.exp(scores - top), axis=-1, keepdims=True))
    probs = jnp.where(allowed, jnp.exp(scores - log_total), 0.0)
    probs_low = probs.astype(BF)
    mixed = (
        jnp.einsum("mgqs,msd->mqgd", probs_low, v, preferred_element_type=F32)
        .astype(BF)
        .reshape(group_rows, q_cols)
    )
    branch_part = dot_right(mixed, wo).astype(BF).reshape(micro, 4, slots, width)
    branch = scatter_yc([branch_part[:, i] for i in range(4)]).reshape(rows, width)

    own_x = tokens.astype(F32).reshape(rows, width)
    first_scale = lax.rsqrt(jnp.mean(own_x * own_x, axis=-1, keepdims=True) + EPS_NORM)
    first_hat = own_x * first_scale
    middle = own_x + branch
    second_scale = lax.rsqrt(jnp.mean(middle * middle, axis=-1, keepdims=True) + EPS_NORM)
    second_hat = middle * second_scale
    second_normalized = (second_hat * gain_two).astype(BF)

    second_normalized, gate_up_mine, down_local = tie(
        second_normalized, gate_up_mine, by_chunk(w_down)
    )
    second_normalized, down_mine = tie(second_normalized, exchange(down_local))
    xn2_around = [second_normalized, ring(second_normalized, size)]
    for s in range(2, size):
        come = ring(xn2_around[-1], size)
        if s == 2:
            come, gate_up_over, down_mine = tie(come, gate_up_over, down_mine)
        xn2_around.append(come)
    down_over = swap(down_mine, "x")
    wgu = put_rows(put_rows(empty_rows(2 * chunk), gate_up_mine, x), gate_up_over, 1 - x)
    wd = put_rows(put_rows(empty_rows(chunk), down_mine, x), down_over, 1 - x)
    wgu = wgu.reshape(width, 2 * chunk)
    wd = wd.reshape(width, chunk)
    xn2_blocks = [b for near in xn2_around for b in (near, swap(near, "y"))]
    dfb_blocks = [b for pair in zip(dfb_around, dfb_over) for b in pair]

    halves = []
    for part in (slice(0, -2), slice(-2, None)):
        xn2 = jnp.concatenate(xn2_blocks[part], axis=0)
        dfb = jnp.concatenate(dfb_blocks[part], axis=0)
        if halves:
            xn2, *halves[0] = tie(xn2, *halves[0])
        gate_up = dot(xn2, wgu)
        gate, up = gate_up[:, :chunk], gate_up[:, chunk:]
        sigmoid = jax.nn.sigmoid(gate)
        activated = gate * sigmoid
        hidden = (activated * up).astype(BF)
        dhid = dot(dfb, wd)
        dgu = jnp.concatenate(
            [
                (dhid * up * sigmoid * (1.0 + gate * (1.0 - sigmoid))).astype(BF),
                (dhid * activated).astype(BF),
            ],
            axis=1,
        )
        if halves:
            ahead = halves[0][4].reshape(size - 1, 2, rows, width)[1]
            first_total = (ahead[0].astype(F32) + swap(ahead[1], "y")).astype(BF)
            first_total, dgu = tie(first_total, dgu)
        dxn2_part = dot_right(dgu, wgu).astype(BF)
        halves.append([xn2, dfb, hidden, dgu, dxn2_part])

    def pieces(parts):
        parts = [p.reshape(-1, 2, rows, width) for p in parts]
        return [[p[s, i] for p in parts for s in range(p.shape[0])] for i in range(2)]

    def over_cores(grad, pieces):
        grad = grad.reshape(size, 2, 2, 2, own_rows, grad.shape[1])
        sums = []
        for i in range(0, size, size // pieces):
            part = grad[i : i + size // pieces]
            sums.append((pick(part, c, 3).astype(F32) + swap(pick(part, 1 - c, 3), "c")).astype(BF))
        return jnp.concatenate(sums, axis=0)

    def over_x(grad):
        total = (pick(grad, x, 1).astype(F32) + swap(pick(grad, 1 - x, 1), "x")).astype(BF)
        return total.reshape(2 * size, own_rows, grad.shape[-1])

    (xn2_a, dfb_a, hidden_a, dgu_a, dxn2_a), (xn2_b, dfb_b, hidden_b, dgu_b, dxn2_b) = halves
    own, away = pieces([dxn2_a, dxn2_b])
    order = [(step + 1) % size for step in range(1, size)]
    away[order[0]], first_total = tie(away[order[0]], first_total)
    got = swap_in_turn([away[s] for s in order], "y")
    dxn2_b, hidden_b, dfb_a, xn2_a = tie(dxn2_b, hidden_b, dfb_a, xn2_a)
    down_grad = (dot_rows(dfb_a, hidden_a) + dot_rows(dfb_b, hidden_b)).astype(BF)
    total = first_total
    for step in range(1, size):
        total = own[order[step - 1]].astype(F32) + got[step - 1] + ring(total, size)
        if step < size - 1:
            total = total.astype(BF)
        if step == 1:
            total, down_grad, xn2_a = tie(total, down_grad, xn2_a)
            down_near = over_cores(down_grad, 2)
            gate_up_grad = dot_rows(xn2_a, dgu_a)
        if step == size - 2:
            total, gate_up_grad = tie(total, gate_up_grad)
            gate_up_grad = (gate_up_grad + dot_rows(xn2_b, dgu_b)).astype(BF)
    feed_a, feed_b = dot_right(hidden_a, wd).astype(BF), dot_right(hidden_b, wd).astype(BF)
    down_sum = over_x(down_near)
    dxn2, gate_up_grad, feed_a, feed_b = tie(total, gate_up_grad, feed_a, feed_b)
    gate_up_near = over_cores(gate_up_grad, 4)

    dh1 = dy + norm_backward(second_hat, second_scale, dxn2 * gain_two)
    dab_blocks = gather_yc(dh1.astype(BF).reshape(micro, slots, width))
    dab_blocks[2], down_sum, gate_up_near = tie(dab_blocks[2], down_sum, gate_up_near)
    gate_up_sum = over_x(gate_up_near)
    down_parts = exchange(down_sum)
    dab_blocks[3], feed_a, feed_b = tie(dab_blocks[3], feed_a, feed_b)
    dab = jnp.concatenate(dab_blocks, axis=1).reshape(group_rows, width)

    def blocks_of(*grads):
        grads = [g.reshape(size, 2, block_rows, g.shape[1]) for g in grads]
        at = [[pick(g, behind(s)) for g in grads] for s in range(size)]
        return [
            [jnp.concatenate([pick(g, i) for g in gs], axis=1) for gs in at] for i in (x, 1 - x)
        ]

    out_grad_part = dot_rows(dab, mixed).astype(BF)

    dob = dot(dab, wo).astype(BF)
    dob = dob.reshape(micro, span, q_heads, HEAD_DIMENSION)
    dprob = jnp.einsum("mqgd,msd->mgqs", dob, v, preferred_element_type=F32)
    dscore = (probs * (dprob - jnp.sum(probs * dprob, axis=-1, keepdims=True))).astype(BF)
    dq = jnp.einsum("mgqs,msd->mqgd", dscore, k, preferred_element_type=F32) * scale
    dk = jnp.einsum("mgqs,mqgd->msd", dscore, q, preferred_element_type=F32) * scale
    dv = jnp.einsum("mgqs,mqgd->msd", probs_low, dob, preferred_element_type=F32)
    dq = rotary_backward(dq, cosine, sine).astype(BF).reshape(group_rows, q_cols)
    dk = rotary_backward(dk[:, :, None, :], cosine, sine).astype(BF).reshape(group_rows, kv_cols)
    dqkv = jnp.concatenate([dq, dk, dv.astype(BF).reshape(group_rows, kv_cols)], axis=1)

    feed = scatter_z(*pieces([feed_a, feed_b]), "y", size)
    outputs = (live * (middle + feed)).astype(BF)
    head_own, head_away = blocks_of(dot_rows(xn1, dqkv).astype(BF), out_grad_part)
    order = [(step + 1) % size for step in range(size)]
    head_away[order[0]], gate_up_sum = tie(head_away[order[0]], gate_up_sum)
    head_got = swap_in_turn([head_away[s] for s in order], "x")
    gate_parts = exchange(gate_up_sum[:, :, :chunk])
    head_got[-1], up_sum = tie(head_got[-1], gate_up_sum[:, :, chunk:])
    up_parts = exchange(up_sum)
    head_sum = head_own[order[0]].astype(F32) + head_got[0]
    for step in range(1, size):
        head_sum = head_sum.astype(BF)
        if step == size - 2:
            head_sum, outputs = tie(head_sum, outputs)
        head_sum = head_own[order[step]].astype(F32) + head_got[step] + ring(head_sum, size)
    outputs = outputs.reshape(hidden_in.shape)

    dxn1_part = dot_right(dqkv, wqkv).astype(BF).reshape(micro, 4, slots, width)
    dxn1 = scatter_yc([dxn1_part[:, i] for i in range(4)]).reshape(rows, width)
    input_grads = (
        (dh1 + norm_backward(first_hat, first_scale, dxn1 * gain_one))
        .astype(BF)
        .reshape(hidden_in.shape)
    )

    def owned(block):
        block = block.astype(BF)
        came = to_peers_yc(lambda k: cut(block, (j ^ k) * own_rows, own_rows, 0))
        heads = jnp.zeros((4, own_rows, block.shape[1]), BF)
        for k in range(4):
            heads = put(heads, came[k], j ^ k)
        return heads

    def side_by_side(parts, start, count):
        return jnp.concatenate(
            [parts[i, :, start : start + count] for i in range(parts.shape[0])], axis=1
        ).astype(F32)

    heads = owned(head_sum)
    grad_query = side_by_side(heads, 0, q_cols)
    grad_key = side_by_side(heads, q_cols, kv_cols)
    grad_value = side_by_side(heads, q_cols + kv_cols, kv_cols)
    grad_out = side_by_side(heads, qkv_cols, q_cols)
    grad_gate = side_by_side(gate_parts, 0, chunk)
    grad_up = side_by_side(up_parts, 0, chunk)
    grad_down = side_by_side(down_parts, 0, chunk)

    def gain_gradient(gain, *pairs):
        total = sum(jnp.sum(w.astype(F32) * g, axis=1) for w, g in pairs)
        return total / gain.astype(F32)

    grad_attn_gain = gain_gradient(
        attn_gain, (w_query, grad_query), (key_matrix, grad_key), (value_matrix, grad_value)
    )
    grad_mlp_gain = gain_gradient(mlp_gain, (w_gate, grad_gate), (w_up, grad_up))
    return (
        outputs,
        input_grads,
        grad_attn_gain,
        grad_query,
        grad_key,
        grad_value,
        grad_out,
        grad_mlp_gain,
        grad_gate,
        grad_up,
        grad_down,
    )


def solution(mesh):
    dp, fsdp = mesh.shape["dp"], mesh.shape["fsdp"]
    fine = Mesh(mesh.devices.reshape(dp // 2, 2, fsdp // 2, 2), ("z", "x", "y", "c"))
    batch, slot, both = ("z", "x"), ("y", "c"), ("z", "x", "y", "c")
    vector, matrix = P(both), P(both, None)
    rows = P(None, batch, slot, None)
    return jax.shard_map(
        per_device,
        mesh=fine,
        in_specs=(rows, P(None, batch), rows) + (vector,) + (matrix,) * 4 + (vector,) + (matrix,) * 3,
        out_specs=(rows, rows, vector) + (matrix,) * 4 + (vector,) + (matrix,) * 3,
        check_vma=False,
    )
```
